32 devices in a mesh: groups: 2 (over y), seq: 16 (over z, x, core).
Axes of the slice: x: 2, y: 2, z: 4, core: 2. Of those that a mesh axis runs over, the one named last changes fastest.
Arguments:
- qkv: bfloat16 [4096, 32, 384], P(('groups', 'seq')), parts along dimension 0
- routes: int32 [4096, 32], P(('groups', 'seq')), parts along dimension 0, may hold values from 0 to 1, as said below
Outputs:
- attended: bfloat16 [4096, 32, 128], P(('groups', 'seq')), parts along dimension 0
The draws below stay inside these ranges and needn't reach their ends.
There are 2 independent parts, one for each index of `groups`. The reference program is written for one: setup_inputs(seed, part) draws one part's arguments, and reference() takes and returns one part's arrays. A program takes and returns all parts, laid end to end along the dimension named above; each array names one. Nothing has to cross between parts.
Inputs may be any that keep to these rules, and one draw needn't show every extreme that they name: Every cluster of every head holds between 512 and 1536 tokens, and in every head some cluster holds exactly 1536. Numbering the pairs (head h, cluster c) as h * 2 + c, the tokens of one device name each aligned group of 4 pairs exactly 256 times. Integer counts, offsets and slot indices derived from routes may cross between devices packed several to a 32-bit word.
All inputs are finite; a program needn't handle non-finite values.
Results may differ from the reference program's by a relative error of at most 0.0047.
Values may be sent and summed in bfloat16 or wider, within the bound.
A program may use at most 128 MiB of HBM per device.

```python
import jax
import jax.numpy as jnp
from jax import lax

H = 32
DH = 128
TOK_DEV = 128
CLEN = 1024
TOKENS = 2048


def draw_routes(key, part):
    ndev = TOKENS // TOK_DEV
    kc = TOKENS // CLEN
    half = kc // 2
    share = CLEN // ndev
    amp = share // 2
    wobble = share // 4
    key_r, key_p, key_z, key_m = jax.random.split(key, 4)
    offsets = jax.random.randint(key_r, (H, half), -amp, amp + 1)
    chosen = jax.random.randint(key_p, (H,), 0, half)
    offsets = jnp.where(jnp.arange(half)[None, :] == chosen[:, None], amp, offsets)
    noise = jax.random.randint(key_z, (ndev, H, half), 0, wobble + 1)
    shifts = offsets[None] + noise - jnp.roll(noise, -1, axis=0)
    sizes = jnp.stack([share + shifts, share - shifts], axis=-1).reshape(ndev * H, kc)
    bounds = jnp.cumsum(sizes, axis=-1)
    ranks = jnp.arange(TOK_DEV, dtype=jnp.int32)
    labels = jax.vmap(lambda edge: jnp.searchsorted(edge, ranks, side='right'))(bounds).astype(jnp.int32)
    orders = jax.vmap(lambda sub: jax.random.permutation(sub, TOK_DEV))(jax.random.split(key_m, ndev * H))
    lines = jnp.arange(ndev * H, dtype=jnp.int32)[:, None]
    placed = jnp.zeros((ndev * H, TOK_DEV), jnp.int32).at[lines, orders].set(labels)
    placed = placed.reshape(ndev, H, TOK_DEV)
    return jnp.transpose(placed, (0, 2, 1)).reshape(TOKENS, H)


def draw_qkv(key, part):
    key_a = jax.random.fold_in(key, 0)
    shape = (TOKENS, H, 3 * DH)
    base = jnp.clip(jax.random.normal(key_a, shape, jnp.float32), -6.0, 6.0)
    return base.astype(jnp.bfloat16)


def setup_inputs(seed: int = 0, part: int = 0) -> dict:
    streams_of = jax.random.split(jax.random.key(seed), 3)
    part_splits = jax.random.split(jax.random.fold_in(streams_of[2], part), 3)
    return {
        "qkv": draw_qkv(jax.random.fold_in(jax.random.fold_in(streams_of[2], part), 71), part),
        "routes": draw_routes(jax.random.fold_in(jax.random.fold_in(streams_of[2], part), 71), part),
    }


def reference(qkv, routes):
    tokens, heads, width = qkv.shape
    head_size = width // 3
    clusters = tokens // CLEN
    capacity = 3 * CLEN // 2
    block_rows = CLEN // 2
    scale = 1.0 / (head_size ** 0.5)
    position = jnp.arange(tokens, dtype=jnp.int32)

    def one_cluster(tile):
        pieces = []
        for index in range(3):
            start = index * block_rows
            stop = start + block_rows
            scores = jnp.dot(tile[start:stop, :head_size], tile[:stop, head_size:2 * head_size].T, preferred_element_type=jnp.float32) * scale
            rows = start + jnp.arange(block_rows, dtype=jnp.int32)[:, None]
            cols = jnp.arange(stop, dtype=jnp.int32)[None, :]
            scores = jnp.where(cols <= rows, scores, -1e30)
            peak = jnp.max(scores, axis=1, keepdims=True)
            expo = jnp.exp(scores - peak)
            weights = (expo / jnp.sum(expo, axis=1, keepdims=True)).astype(jnp.bfloat16)
            pieces.append(jnp.dot(weights, tile[:stop, 2 * head_size:], preferred_element_type=jnp.float32).astype(jnp.bfloat16))
        return jnp.concatenate(pieces, axis=0)

    def one_head(head):
        labels = routes[:, head].astype(jnp.int32)
        order = jnp.argsort(labels * tokens + position).astype(jnp.int32)
        sorted_labels = labels[order]
        counts = jax.ops.segment_sum(jnp.ones((tokens,), jnp.int32), labels, clusters)
        starts = (jnp.cumsum(counts) - counts).astype(jnp.int32)
        slots = position - starts[sorted_labels]
        rows = qkv[:, head, :][order]
        tiles = jnp.zeros((clusters, capacity, width), jnp.bfloat16).at[sorted_labels, slots].set(rows)
        results = lax.map(one_cluster, tiles)
        back = results[sorted_labels, slots]
        return jnp.zeros((tokens, head_size), jnp.bfloat16).at[order].set(back)

    outputs = lax.map(one_head, jnp.arange(heads, dtype=jnp.int32))
    return jnp.transpose(outputs, (1, 0, 2))
```

```python
import functools
import math

import jax
import jax.numpy as jnp
from jax import lax
from jax.experimental import pallas as pl
from jax.experimental.pallas import tpu as pltpu
from jax.sharding import PartitionSpec as P

CLEN = 1024
LABEL_ROWS = 8
NEG = -1e30


def entering(part, axis, combine, identity):
    place = lax.axis_index(axis)
    gathered = lax.all_gather(part, axis)
    state = jnp.zeros_like(part) + jnp.asarray(identity, part.dtype)

    def one(turn, state):
        return combine(state, lax.dynamic_index_in_dim(gathered, turn, 0, False))

    return lax.fori_loop(0, place, one, state)


def attend(queries, keys, values, start, scale):
    block_rows = queries.shape[1]
    span = keys.shape[1]
    scores = jnp.einsum("pqd,pkd->pqk", queries, keys, preferred_element_type=jnp.float32) * scale
    rows = start + jnp.arange(block_rows, dtype=jnp.int32)[:, None]
    cols = jnp.arange(span, dtype=jnp.int32)[None, :]
    scores = jnp.where((cols <= rows)[None], scores, -1e30)
    peak = jnp.max(scores, axis=2, keepdims=True)
    expo = jnp.exp(scores - peak)
    weights = (expo / jnp.sum(expo, axis=2, keepdims=True)).astype(jnp.bfloat16)
    return jnp.einsum("pqk,pkd->pqd", weights, values, preferred_element_type=jnp.float32).astype(
        jnp.bfloat16
    )


def routed(qkv, routes):
    tok, heads, width = qkv.shape
    head_size = width // 3
    nseq = lax.axis_size("seq")
    clusters = nseq * tok // CLEN
    pairs_dev = heads * tok // CLEN
    capacity = 3 * CLEN // 2
    block_rows = CLEN // 2
    share = CLEN // nseq
    rows_peer = pairs_dev * share
    total_pairs = heads * clusters
    scale = 1.0 / math.sqrt(head_size)
    member = routes[:, :, None] == jnp.arange(clusters, dtype=jnp.int32)[None, None, :]
    member_flat = member.reshape(tok, total_pairs)
    counts = jnp.sum(member_flat.astype(jnp.int32), axis=0)
    earlier = (jnp.arange(tok)[:, None] > jnp.arange(tok)[None, :]).astype(jnp.bfloat16)
    before = jnp.dot(earlier, member_flat.astype(jnp.bfloat16), preferred_element_type=jnp.float32)
    rank = jnp.sum(jnp.where(member, before.reshape(tok, heads, clusters), 0.0), axis=2).astype(
        jnp.int32
    )
    prefix = entering(counts, "seq", lambda first, second: first + second, jnp.zeros_like(counts))

    def lookup(table):
        return jnp.sum(jnp.where(member, table.reshape(heads, clusters)[None], 0), axis=2)

    group_counts = counts.reshape(total_pairs // pairs_dev, pairs_dev)
    within = (jnp.cumsum(group_counts, axis=1) - group_counts).reshape(total_pairs)
    slot = lookup(prefix) + rank
    pair_index = jnp.arange(heads, dtype=jnp.int32)[None, :] * clusters + routes
    owner = pair_index // pairs_dev
    local_pair = pair_index % pairs_dev
    position = (owner * rows_peer + lookup(within) + rank).reshape(tok * heads)
    target = (local_pair * capacity + slot).reshape(tok * heads)
    outgoing = (
        jnp.zeros((tok * heads, width), jnp.bfloat16)
        .at[position]
        .set(qkv.reshape(tok * heads, width))
    )
    labels = jnp.zeros((tok * heads,), jnp.int32).at[position].set(target)
    arrived, places = (
        lax.all_to_all(outgoing, "seq", split_axis=0, concat_axis=0, tiled=True),
        lax.all_to_all(labels, "seq", split_axis=0, concat_axis=0, tiled=True),
    )
    tiles = jnp.zeros((pairs_dev * capacity, width), jnp.bfloat16).at[places].set(arrived)
    tiles = tiles.reshape(pairs_dev, capacity, width)
    pieces = []
    for index in range(3):
        start = index * block_rows
        stop = start + block_rows
        pieces.append(
            attend(
                tiles[:, start:stop, :head_size],
                tiles[:, :stop, head_size : 2 * head_size],
                tiles[:, :stop, 2 * head_size :],
                start,
                scale,
            )
        )
    results = jnp.concatenate(pieces, axis=1)
    flat_results = results.reshape(pairs_dev * capacity, head_size)
    replies = flat_results[places]
    returned = lax.all_to_all(replies, "seq", split_axis=0, concat_axis=0, tiled=True)
    return returned[position].reshape(tok, heads, head_size)


def softmax_block(query, keys, values, lab_col, lab_row, scale):
    rows, head_size = query.shape
    span = keys.shape[0]
    contract = (((1,), (1,)), ((), ()))
    scores = lax.dot_general(query, keys, contract, preferred_element_type=jnp.float32)
    same = lab_col == lab_row
    past = span - rows
    row_id = lax.broadcasted_iota(jnp.int32, (rows, rows), 0)
    col_id = lax.broadcasted_iota(jnp.int32, (rows, rows), 1)
    last = jnp.where(same[:, past:] & (col_id <= row_id), scores[:, past:], NEG)
    if past:
        first = jnp.where(same[:, :past], scores[:, :past], NEG)
        scores = jnp.concatenate([first, last], axis=1)
    else:
        scores = last
    factor = scale * math.log2(math.e)
    peak = jnp.max(scores, axis=1, keepdims=True) * factor
    expo = jnp.exp2(scores * factor - peak)
    total = jnp.sum(expo, axis=1, keepdims=True)
    out = jnp.dot(expo.astype(jnp.bfloat16), values, preferred_element_type=jnp.float32)
    return (out / total).astype(jnp.bfloat16)


def exchange_kernel(
    nseq, held, group, x_ref, lab_ref, out_ref, recv, labs, obuf, cols,
    x_send, x_recv, l_send, l_recv, o_send, o_recv, own_sem,
):
    me = lax.axis_index("seq")
    tok, width = x_ref.shape[1:]
    size = width // 3
    scale = 1.0 / math.sqrt(size)
    rows = group * tok

    def peer_of(k):
        return lax.rem(me + k, nseq)

    def x_copy(j, peer):
        return pltpu.make_async_remote_copy(
            src_ref=x_ref.at[peer * held + j], dst_ref=recv.at[j, me],
            send_sem=x_send.at[j, peer], recv_sem=x_recv.at[j, me],
            device_id={"seq": peer}, device_id_type=pl.DeviceIdType.MESH,
        )

    def x_arrival(j, source):
        return pltpu.make_async_remote_copy(
            src_ref=x_ref.at[0], dst_ref=recv.at[j, source],
            send_sem=x_send.at[j, source], recv_sem=x_recv.at[j, source],
            device_id={"seq": source}, device_id_type=pl.DeviceIdType.MESH,
        )

    def l_copy(peer):
        return pltpu.make_async_remote_copy(
            src_ref=lab_ref.at[peer], dst_ref=labs.at[me],
            send_sem=l_send.at[peer], recv_sem=l_recv.at[me],
            device_id={"seq": peer}, device_id_type=pl.DeviceIdType.MESH,
        )

    def l_arrival(source):
        return pltpu.make_async_remote_copy(
            src_ref=lab_ref.at[0], dst_ref=labs.at[source],
            send_sem=l_send.at[source], recv_sem=l_recv.at[source],
            device_id={"seq": source}, device_id_type=pl.DeviceIdType.MESH,
        )

    def o_copy(j, peer):
        return pltpu.make_async_remote_copy(
            src_ref=obuf.at[j, peer], dst_ref=out_ref.at[me * held + j],
            send_sem=o_send.at[j, peer], recv_sem=o_recv.at[j, me],
            device_id={"seq": peer}, device_id_type=pl.DeviceIdType.MESH,
        )

    def o_arrival(j, source):
        return pltpu.make_async_remote_copy(
            src_ref=obuf.at[j, 0], dst_ref=out_ref.at[source * held + j],
            send_sem=o_send.at[j, source], recv_sem=o_recv.at[j, source],
            device_id={"seq": source}, device_id_type=pl.DeviceIdType.MESH,
        )

    def own_x(j):
        return pltpu.make_async_copy(x_ref.at[me * held + j], recv.at[j, me], own_sem.at[j])

    def own_o(j):
        return pltpu.make_async_copy(
            obuf.at[j, me], out_ref.at[me * held + j], own_sem.at[held + 1 + j]
        )

    own_l = pltpu.make_async_copy(lab_ref.at[me], labs.at[me], own_sem.at[held])

    def each_peer(body):
        def step(k, carry):
            body(peer_of(k))
            return carry

        lax.fori_loop(1, nseq, step, 0)

    own_l.start()
    for j in range(held):
        own_x(j).start()
    barrier = pltpu.get_barrier_semaphore()
    each_peer(lambda peer: pl.semaphore_signal(
        barrier, inc=1, device_id={"seq": peer}, device_id_type=pl.DeviceIdType.MESH))
    pl.semaphore_wait(barrier, nseq - 1)

    def start_first(peer):
        l_copy(peer).start()
        x_copy(0, peer).start()

    each_peer(start_first)
    own_l.wait()
    each_peer(lambda peer: l_arrival(peer).wait_recv())
    for j in range(held):
        own_x(j).wait()

    eye = lax.broadcasted_iota(jnp.int32, (tok, tok), 0) == lax.broadcasted_iota(
        jnp.int32, (tok, tok), 1)

    for j in range(held):
        for source in range(nseq):
            line = labs[source, j : j + 1, :]
            cols[j, source * tok : (source + 1) * tok, :] = jnp.sum(
                jnp.where(eye, line, 0), axis=1, keepdims=True)

    for j in range(held):
        if j + 1 < held:
            def forward(peer):
                x_copy(j, peer).wait_send()
                x_copy(j + 1, peer).start()

            each_peer(forward)
        for block in range(nseq // group):
            sources = range(block * group, (block + 1) * group)
            for source in sources:
                @pl.when(me != source)
                def _():
                    x_arrival(j, source).wait_recv()
            span = (block + 1) * group
            query = recv[j, block * group : span, :, :size].reshape(rows, size)
            keys = recv[j, :span, :, size : 2 * size].reshape(span * tok, size)
            values = recv[j, :span, :, 2 * size :].reshape(span * tok, size)
            lab_row = jnp.concatenate([labs[s, j : j + 1, :] for s in range(span)], axis=1)
            lab_col = cols[j, block * rows : (block + 1) * rows, :]
            result = softmax_block(query, keys, values, lab_col, lab_row, scale)
            obuf[j, block * group : span] = result.reshape(group, tok, size)
            for source in sources:
                @pl.when(me != source)
                def _():
                    o_copy(j, source).start()

                @pl.when(me == source)
                def _():
                    own_o(j).start()

    each_peer(lambda peer: l_copy(peer).wait_send())
    each_peer(lambda peer: x_copy(held - 1, peer).wait_send())
    for j in range(held):
        own_o(j).wait()

        def finish(peer):
            o_copy(j, peer).wait_send()
            o_arrival(j, peer).wait_recv()

        each_peer(finish)


def by_head(qkv, routes):
    tok, heads, width = qkv.shape
    size = width // 3
    nseq = lax.axis_size("seq")
    held = heads // nseq
    group = 2 if nseq % 2 == 0 else 1
    lines = jnp.transpose(routes, (1, 0)).reshape(nseq, held, tok)
    lines = jnp.pad(lines, ((0, 0), (0, LABEL_ROWS - held), (0, 0)))
    dma = pltpu.SemaphoreType.DMA
    out = pl.pallas_call(
        functools.partial(exchange_kernel, nseq, held, group),
        out_shape=jax.ShapeDtypeStruct((heads, tok, size), jnp.bfloat16),
        in_specs=[pl.BlockSpec(memory_space=pl.ANY)] * 2,
        out_specs=pl.BlockSpec(memory_space=pl.ANY),
        scratch_shapes=[
            pltpu.VMEM((held, nseq, tok, width), jnp.bfloat16),
            pltpu.VMEM((nseq, LABEL_ROWS, tok), jnp.int32),
            pltpu.VMEM((held, nseq, tok, size), jnp.bfloat16),
            pltpu.VMEM((held, nseq * tok, 1), jnp.int32),
            dma((held, nseq)),
            dma((held, nseq)),
            dma((nseq,)),
            dma((nseq,)),
            dma((held, nseq)),
            dma((held, nseq)),
            dma((2 * held + 1,)),
        ],
        compiler_params=pltpu.CompilerParams(
            collective_id=0, has_side_effects=True, vmem_limit_bytes=48 * 2**20
        ),
        name="exchange",
    )(jnp.transpose(qkv, (1, 0, 2)), lines)
    return jnp.transpose(out, (1, 0, 2))


def solution(mesh):
    placed = (P(("groups", "seq"), None, None), P(("groups", "seq"), None))
    nseq = mesh.shape["seq"]

    def local(qkv, routes):
        heads = qkv.shape[1]
        if heads % nseq == 0 and heads // nseq <= LABEL_ROWS:
            return by_head(qkv, routes)
        return routed(qkv, routes)

    return jax.shard_map(
        local,
        mesh=mesh,
        in_specs=placed,
        out_specs=P(("groups", "seq"), None, None),
        check_vma=False,
    )
```

```python
import functools
import math

import jax
import jax.numpy as jnp
from jax import lax
from jax.experimental import pallas as pl
from jax.experimental.pallas import tpu as pltpu
from jax.sharding import PartitionSpec as P

CLEN = 1024
LABEL_ROWS = 8
NEG = -1e30


def entering(part, axis, combine, identity):
    place = lax.axis_index(axis)
    gathered = lax.all_gather(part, axis)
    state = jnp.zeros_like(part) + jnp.asarray(identity, part.dtype)

    def one(turn, state):
        return combine(state, lax.dynamic_index_in_dim(gathered, turn, 0, False))

    return lax.fori_loop(0, place, one, state)


def attend(queries, keys, values, start, scale):
    block_rows = queries.shape[1]
    span = keys.shape[1]
    scores = jnp.einsum("pqd,pkd->pqk", queries, keys, preferred_element_type=jnp.float32) * scale
    rows = start + jnp.arange(block_rows, dtype=jnp.int32)[:, None]
    cols = jnp.arange(span, dtype=jnp.int32)[None, :]
    scores = jnp.where((cols <= rows)[None], scores, -1e30)
    peak = jnp.max(scores, axis=2, keepdims=True)
    expo = jnp.exp(scores - peak)
    weights = (expo / jnp.sum(expo, axis=2, keepdims=True)).astype(jnp.bfloat16)
    return jnp.einsum("pqk,pkd->pqd", weights, values, preferred_element_type=jnp.float32).astype(
        jnp.bfloat16
    )


def routed(qkv, routes):
    tok, heads, width = qkv.shape
    head_size = width // 3
    nseq = lax.axis_size("seq")
    clusters = nseq * tok // CLEN
    pairs_dev = heads * tok // CLEN
    capacity = 3 * CLEN // 2
    block_rows = CLEN // 2
    share = CLEN // nseq
    rows_peer = pairs_dev * share
    total_pairs = heads * clusters
    scale = 1.0 / math.sqrt(head_size)
    member = routes[:, :, None] == jnp.arange(clusters, dtype=jnp.int32)[None, None, :]
    member_flat = member.reshape(tok, total_pairs)
    counts = jnp.sum(member_flat.astype(jnp.int32), axis=0)
    earlier = (jnp.arange(tok)[:, None] > jnp.arange(tok)[None, :]).astype(jnp.bfloat16)
    before = jnp.dot(earlier, member_flat.astype(jnp.bfloat16), preferred_element_type=jnp.float32)
    rank = jnp.sum(jnp.where(member, before.reshape(tok, heads, clusters), 0.0), axis=2).astype(
        jnp.int32
    )
    prefix = entering(counts, "seq", lambda first, second: first + second, jnp.zeros_like(counts))

    def lookup(table):
        return jnp.sum(jnp.where(member, table.reshape(heads, clusters)[None], 0), axis=2)

    group_counts = counts.reshape(total_pairs // pairs_dev, pairs_dev)
    within = (jnp.cumsum(group_counts, axis=1) - group_counts).reshape(total_pairs)
    slot = lookup(prefix) + rank
    pair_index = jnp.arange(heads, dtype=jnp.int32)[None, :] * clusters + routes
    owner = pair_index // pairs_dev
    local_pair = pair_index % pairs_dev
    position = (owner * rows_peer + lookup(within) + rank).reshape(tok * heads)
    target = (local_pair * capacity + slot).reshape(tok * heads)
    outgoing = (
        jnp.zeros((tok * heads, width), jnp.bfloat16)
        .at[position]
        .set(qkv.reshape(tok * heads, width))
    )
    labels = jnp.zeros((tok * heads,), jnp.int32).at[position].set(target)
    arrived, places = (
        lax.all_to_all(outgoing, "seq", split_axis=0, concat_axis=0, tiled=True),
        lax.all_to_all(labels, "seq", split_axis=0, concat_axis=0, tiled=True),
    )
    tiles = jnp.zeros((pairs_dev * capacity, width), jnp.bfloat16).at[places].set(arrived)
    tiles = tiles.reshape(pairs_dev, capacity, width)
    pieces = []
    for index in range(3):
        start = index * block_rows
        stop = start + block_rows
        pieces.append(
            attend(
                tiles[:, start:stop, :head_size],
                tiles[:, :stop, head_size : 2 * head_size],
                tiles[:, :stop, 2 * head_size :],
                start,
                scale,
            )
        )
    results = jnp.concatenate(pieces, axis=1)
    flat_results = results.reshape(pairs_dev * capacity, head_size)
    replies = flat_results[places]
    returned = lax.all_to_all(replies, "seq", split_axis=0, concat_axis=0, tiled=True)
    return returned[position].reshape(tok, heads, head_size)


def partial_softmax(query, keys, values, lab_col, lab_row, scale, causal):
    rows, head_size = query.shape
    span = keys.shape[0]
    contract = (((1,), (1,)), ((), ()))
    scores = lax.dot_general(query, keys, contract, preferred_element_type=jnp.float32)
    same = lab_col == lab_row
    if causal:
        past = span - rows
        row_id = lax.broadcasted_iota(jnp.int32, (rows, rows), 0)
        col_id = lax.broadcasted_iota(jnp.int32, (rows, rows), 1)
        last = jnp.where(same[:, past:] & (col_id <= row_id), scores[:, past:], NEG)
        if past:
            first = jnp.where(same[:, :past], scores[:, :past], NEG)
            scores = jnp.concatenate([first, last], axis=1)
        else:
            scores = last
    else:
        scores = jnp.where(same, scores, NEG)
    factor = scale * math.log2(math.e)
    peak = jnp.max(scores, axis=1, keepdims=True) * factor
    expo = jnp.exp2(scores * factor - peak)
    total = jnp.sum(expo, axis=1, keepdims=True)
    out = jnp.dot(expo.astype(jnp.bfloat16), values, preferred_element_type=jnp.float32)
    return (out / total).astype(jnp.bfloat16), peak, total


def exchange_kernel(
    nseq, held, group, x_ref, lab_ref, out_ref, recv, qrecv, labs, obuf, sbuf, part, stats, merged, cols,
    x_send, x_recv, q_send, q_recv, l_send, l_recv, o_send, o_recv, s_send, s_recv,
    own_x, own_l, own_o, own_s, m_sem,
):
    me = lax.axis_index("seq")
    half = nseq // 2
    low = me < half
    up = me >= half
    side = me // half
    base = side * half
    mine = lax.rem(me, half)
    tok, width = x_ref.shape[1:]
    size = width // 3
    scale = 1.0 / math.sqrt(size)
    rows = group * tok

    def remote(src, dst, send, recv_sem, peer):
        return pltpu.make_async_remote_copy(
            src_ref=src, dst_ref=dst, send_sem=send, recv_sem=recv_sem,
            device_id={"seq": peer}, device_id_type=pl.DeviceIdType.MESH,
        )

    def x_copy(j, p):
        return remote(x_ref.at[p * held + j], recv.at[j, mine],
                      x_send.at[j, p], x_recv.at[j, mine], base + p)

    def x_arrival(j, p):
        return remote(x_ref.at[0], recv.at[j, p], x_send.at[j, p], x_recv.at[j, p], base + p)

    def q_copy(j, p):
        return remote(x_ref.at[p * held + j, :, pl.ds(0, size)], qrecv.at[j, mine],
                      q_send.at[j, p], q_recv.at[j, mine], p)

    def q_arrival(j, p):
        return remote(x_ref.at[0, :, pl.ds(0, size)], qrecv.at[j, p],
                      q_send.at[j, p], q_recv.at[j, p], half + p)

    def l_copy(peer):
        return remote(lab_ref.at[lax.rem(peer, half)], labs.at[me],
                      l_send.at[peer], l_recv.at[me], peer)

    def l_arrival(peer):
        return remote(lab_ref.at[0], labs.at[peer], l_send.at[peer], l_recv.at[peer], peer)

    def o_copy_low(j, p):
        return remote(obuf.at[j, p], out_ref.at[mine * held + j],
                      o_send.at[j, p], o_recv.at[0, j, mine], p)

    def o_arrival_low(j, p):
        return remote(obuf.at[j, 0], out_ref.at[p * held + j],
                      o_send.at[j, p], o_recv.at[0, j, p], p)

    def o_copy_up(j, peer):
        return remote(obuf.at[j, peer], part.at[side, mine * held + j],
                      o_send.at[j, peer], o_recv.at[side, j, mine], peer)

    def o_arrival_up(which, j, p):
        return remote(obuf.at[j, 0], part.at[which, p * held + j],
                      o_send.at[j, which * half + p], o_recv.at[which, j, p], which * half + p)

    def s_copy(j, peer):
        return remote(sbuf.at[j, peer], stats.at[side, mine, j],
                      s_send.at[j, peer], s_recv.at[side, j, mine], peer)

    def s_arrival(which, j, p):
        return remote(sbuf.at[j, 0], stats.at[which, p, j],
                      s_send.at[j, which * half + p], s_recv.at[which, j, p], which * half + p)

    def own_x_copy(j):
        return pltpu.make_async_copy(x_ref.at[mine * held + j], recv.at[j, mine], own_x.at[j])

    def own_o_low(j):
        return pltpu.make_async_copy(obuf.at[j, me], out_ref.at[mine * held + j], own_o.at[j])

    def own_o_up(j):
        return pltpu.make_async_copy(obuf.at[j, me], part.at[1, mine * held + j], own_o.at[j])

    def own_s_up(j):
        return pltpu.make_async_copy(sbuf.at[j, me], stats.at[1, mine, j], own_s.at[j])

    def result_copy(head):
        return pltpu.make_async_copy(merged.at[head], out_ref.at[head], m_sem.at[head])

    own_lab = pltpu.make_async_copy(lab_ref.at[mine], labs.at[me], own_l.at[0])

    def loop(start, stop, body):
        def step(k, carry):
            body(k)
            return carry

        lax.fori_loop(start, stop, step, 0)

    def each_peer(body):
        loop(1, nseq, lambda k: body(lax.rem(me + k, nseq)))

    def each_near(body):
        loop(1, half, lambda k: body(lax.rem(mine + k, half)))

    def each_far(body):
        loop(0, half, lambda k: body(lax.rem(mine + k, half)))

    own_lab.start()
    for j in range(held):
        own_x_copy(j).start()
    barrier = pltpu.get_barrier_semaphore()
    each_peer(lambda peer: pl.semaphore_signal(
        barrier, inc=1, device_id={"seq": peer}, device_id_type=pl.DeviceIdType.MESH))
    pl.semaphore_wait(barrier, nseq - 1)

    each_near(lambda p: l_copy(base + p).start())

    @pl.when(up)
    def _():
        each_far(lambda p: l_copy(p).start())
        each_far(lambda p: q_copy(0, p).start())

    each_near(lambda p: x_copy(0, p).start())
    own_lab.wait()
    for j in range(held):
        own_x_copy(j).wait()
    each_near(lambda p: l_arrival(base + p).wait_recv())

    @pl.when(low)
    def _():
        each_far(lambda p: l_arrival(half + p).wait_recv())

    eye = lax.broadcasted_iota(jnp.int32, (tok, tok), 0) == lax.broadcasted_iota(
        jnp.int32, (tok, tok), 1)

    def to_col(line):
        return jnp.sum(jnp.where(eye, line, jnp.zeros_like(line)), axis=1, keepdims=True)

    def to_row(col):
        return jnp.sum(jnp.where(eye, col, jnp.zeros_like(col)), axis=0, keepdims=True)

    def keep(j, first, block, result, peak, total):
        for g in range(group):
            source = first + block * group + g
            obuf[j, source] = result[g * tok : (g + 1) * tok]
            sbuf[j, source, 0:1, :] = to_row(peak[g * tok : (g + 1) * tok])
            sbuf[j, source, 1:2, :] = to_row(total[g * tok : (g + 1) * tok])

    def chunk(j):
        @pl.when(j + 1 < held)
        def _():
            @pl.when(up)
            def _():
                def forward_q(p):
                    q_copy(j, p).wait_send()
                    q_copy(j + 1, p).start()

                each_far(forward_q)

            def forward_x(p):
                x_copy(j, p).wait_send()
                x_copy(j + 1, p).start()

            each_near(forward_x)

        def fill_cols(p):
            cols[base + p] = to_col(labs[base + p, pl.ds(j, 1), :])

        loop(0, half, fill_cols)

        @pl.when(low)
        def _():
            def fill_far(p):
                cols[half + p] = to_col(labs[half + p, pl.ds(j, 1), :])

            loop(0, half, fill_far)

        for block in range(half // group):
            for g in range(group):
                p = block * group + g

                @pl.when(mine != p)
                def _():
                    x_arrival(j, p).wait_recv()

            span = (block + 1) * group
            query = recv[j, block * group : span, :, :size].reshape(rows, size)
            keys = recv[j, :span, :, size : 2 * size].reshape(span * tok, size)
            values = recv[j, :span, :, 2 * size :].reshape(span * tok, size)
            lab_row = jnp.concatenate(
                [labs[base + p, pl.ds(j, 1), :] for p in range(span)], axis=1)
            lab_col = jnp.concatenate(
                [cols[base + block * group + g] for g in range(group)], axis=0)
            result, peak, total = partial_softmax(
                query, keys, values, lab_col, lab_row, scale, True)
            keep(j, base, block, result, peak, total)
            for g in range(group):
                p = block * group + g

                @pl.when(low & (mine != p))
                def _():
                    o_copy_low(j, p).start()

                @pl.when(low & (mine == p))
                def _():
                    own_o_low(j).start()

                @pl.when(up & (mine != p))
                def _():
                    o_copy_up(j, half + p).start()
                    s_copy(j, half + p).start()

                @pl.when(up & (mine == p))
                def _():
                    own_o_up(j).start()
                    own_s_up(j).start()

        @pl.when(low)
        def _():
            for block in range(half // group):
                for g in range(group):
                    q_arrival(j, block * group + g).wait_recv()
                query = qrecv[j, block * group : (block + 1) * group].reshape(rows, size)
                keys = recv[j, :, :, size : 2 * size].reshape(half * tok, size)
                values = recv[j, :, :, 2 * size :].reshape(half * tok, size)
                lab_row = jnp.concatenate(
                    [labs[p, pl.ds(j, 1), :] for p in range(half)], axis=1)
                lab_col = jnp.concatenate(
                    [cols[half + block * group + g] for g in range(group)], axis=0)
                result, peak, total = partial_softmax(
                    query, keys, values, lab_col, lab_row, scale, False)
                keep(j, half, block, result, peak, total)
                for g in range(group):
                    o_copy_up(j, half + block * group + g).start()
                    s_copy(j, half + block * group + g).start()

    loop(0, held, chunk)

    each_near(lambda p: l_copy(base + p).wait_send())
    each_near(lambda p: x_copy(held - 1, p).wait_send())

    @pl.when(low)
    def _():
        def finish(j):
            own_o_low(j).wait()

            def near(p):
                o_copy_low(j, p).wait_send()
                o_arrival_low(j, p).wait_recv()

            def far(p):
                o_copy_up(j, half + p).wait_send()
                s_copy(j, half + p).wait_send()

            each_near(near)
            each_far(far)

        loop(0, held, finish)

    @pl.when(up)
    def _():
        each_far(lambda p: l_copy(p).wait_send())
        each_far(lambda p: q_copy(held - 1, p).wait_send())

        def finish(j):
            own_o_up(j).wait()
            own_s_up(j).wait()

            def near(p):
                o_copy_up(j, half + p).wait_send()
                s_copy(j, half + p).wait_send()
                o_arrival_up(1, j, p).wait_recv()
                s_arrival(1, j, p).wait_recv()

            each_near(near)

            def merge(p):
                o_arrival_up(0, j, p).wait_recv()
                s_arrival(0, j, p).wait_recv()
                head = p * held + j
                peak0, peak1 = stats[0, p, j, 0:1, :], stats[1, p, j, 0:1, :]
                peak = jnp.maximum(peak0, peak1)
                weight0 = stats[0, p, j, 1:2, :] * jnp.exp2(peak0 - peak)
                weight1 = stats[1, p, j, 1:2, :] * jnp.exp2(peak1 - peak)
                total = weight0 + weight1
                merged[head] = (
                    to_col(weight0 / total) * part[0, head].astype(jnp.float32)
                    + to_col(weight1 / total) * part[1, head].astype(jnp.float32)
                ).astype(jnp.bfloat16)
                result_copy(head).start()

            loop(0, half, merge)

        loop(0, held, finish)
        loop(0, half * held, lambda head: result_copy(head).wait())


def by_head(qkv, routes):
    tok, heads, width = qkv.shape
    size = width // 3
    nseq = lax.axis_size("seq")
    half = nseq // 2
    held = heads // half
    group = 2 if half % 2 == 0 else 1
    lines = jnp.transpose(routes, (1, 0)).reshape(half, held, tok)
    lines = jnp.pad(lines, ((0, 0), (0, LABEL_ROWS - held), (0, 0)))
    dma = pltpu.SemaphoreType.DMA
    out = pl.pallas_call(
        functools.partial(exchange_kernel, nseq, held, group),
        out_shape=jax.ShapeDtypeStruct((heads, tok, size), jnp.bfloat16),
        in_specs=[pl.BlockSpec(memory_space=pl.ANY)] * 2,
        out_specs=pl.BlockSpec(memory_space=pl.ANY),
        scratch_shapes=[
            pltpu.VMEM((held, half, tok, width), jnp.bfloat16),
            pltpu.VMEM((held, half, tok, size), jnp.bfloat16),
            pltpu.VMEM((nseq, LABEL_ROWS, tok), jnp.int32),
            pltpu.VMEM((held, nseq, tok, size), jnp.bfloat16),
            pltpu.VMEM((held, nseq, 8, tok), jnp.float32),
            pltpu.VMEM((2, heads, tok, size), jnp.bfloat16),
            pltpu.VMEM((2, half, held, 8, tok), jnp.float32),
            pltpu.VMEM((heads, tok, size), jnp.bfloat16),
            pltpu.VMEM((nseq, tok, 1), jnp.int32),
            dma((held, half)),
            dma((held, half)),
            dma((held, half)),
            dma((held, half)),
            dma((nseq,)),
            dma((nseq,)),
            dma((held, nseq)),
            dma((2, held, half)),
            dma((held, nseq)),
            dma((2, held, half)),
            dma((held,)),
            dma((1,)),
            dma((held,)),
            dma((held,)),
            dma((heads,)),
        ],
        compiler_params=pltpu.CompilerParams(
            collective_id=0, has_side_effects=True, vmem_limit_bytes=48 * 2**20
        ),
        name="exchange",
    )(jnp.transpose(qkv, (1, 0, 2)), lines)
    return jnp.transpose(out, (1, 0, 2))


def solution(mesh):
    placed = (P(("groups", "seq"), None, None), P(("groups", "seq"), None))
    nseq = mesh.shape["seq"]

    def local(qkv, routes):
        heads = qkv.shape[1]
        half = nseq // 2
        if nseq % 2 == 0 and heads % half == 0 and heads // half <= LABEL_ROWS:
            return by_head(qkv, routes)
        return routed(qkv, routes)

    return jax.shard_map(
        local,
        mesh=mesh,
        in_specs=placed,
        out_specs=P(("groups", "seq"), None, None),
        check_vma=False,
    )
```

```python
import functools
import math

import jax
import jax.numpy as jnp
from jax import lax
from jax.experimental import pallas as pl
from jax.experimental.pallas import tpu as pltpu
from jax.sharding import PartitionSpec as P

CLEN = 1024
LABEL_ROWS = 8
NEG = -1e30


def entering(part, axis, combine, identity):
    place = lax.axis_index(axis)
    gathered = lax.all_gather(part, axis)
    state = jnp.zeros_like(part) + jnp.asarray(identity, part.dtype)

    def one(turn, state):
        return combine(state, lax.dynamic_index_in_dim(gathered, turn, 0, False))

    return lax.fori_loop(0, place, one, state)


def attend(queries, keys, values, start, scale):
    block_rows = queries.shape[1]
    span = keys.shape[1]
    scores = jnp.einsum("pqd,pkd->pqk", queries, keys, preferred_element_type=jnp.float32) * scale
    rows = start + jnp.arange(block_rows, dtype=jnp.int32)[:, None]
    cols = jnp.arange(span, dtype=jnp.int32)[None, :]
    scores = jnp.where((cols <= rows)[None], scores, -1e30)
    peak = jnp.max(scores, axis=2, keepdims=True)
    expo = jnp.exp(scores - peak)
    weights = (expo / jnp.sum(expo, axis=2, keepdims=True)).astype(jnp.bfloat16)
    return jnp.einsum("pqk,pkd->pqd", weights, values, preferred_element_type=jnp.float32).astype(
        jnp.bfloat16
    )


def routed(qkv, routes):
    tok, heads, width = qkv.shape
    head_size = width // 3
    nseq = lax.axis_size("seq")
    clusters = nseq * tok // CLEN
    pairs_dev = heads * tok // CLEN
    capacity = 3 * CLEN // 2
    block_rows = CLEN // 2
    share = CLEN // nseq
    rows_peer = pairs_dev * share
    total_pairs = heads * clusters
    scale = 1.0 / math.sqrt(head_size)
    member = routes[:, :, None] == jnp.arange(clusters, dtype=jnp.int32)[None, None, :]
    member_flat = member.reshape(tok, total_pairs)
    counts = jnp.sum(member_flat.astype(jnp.int32), axis=0)
    earlier = (jnp.arange(tok)[:, None] > jnp.arange(tok)[None, :]).astype(jnp.bfloat16)
    before = jnp.dot(earlier, member_flat.astype(jnp.bfloat16), preferred_element_type=jnp.float32)
    rank = jnp.sum(jnp.where(member, before.reshape(tok, heads, clusters), 0.0), axis=2).astype(
        jnp.int32
    )
    prefix = entering(counts, "seq", lambda first, second: first + second, jnp.zeros_like(counts))

    def lookup(table):
        return jnp.sum(jnp.where(member, table.reshape(heads, clusters)[None], 0), axis=2)

    group_counts = counts.reshape(total_pairs // pairs_dev, pairs_dev)
    within = (jnp.cumsum(group_counts, axis=1) - group_counts).reshape(total_pairs)
    slot = lookup(prefix) + rank
    pair_index = jnp.arange(heads, dtype=jnp.int32)[None, :] * clusters + routes
    owner = pair_index // pairs_dev
    local_pair = pair_index % pairs_dev
    position = (owner * rows_peer + lookup(within) + rank).reshape(tok * heads)
    target = (local_pair * capacity + slot).reshape(tok * heads)
    outgoing = (
        jnp.zeros((tok * heads, width), jnp.bfloat16)
        .at[position]
        .set(qkv.reshape(tok * heads, width))
    )
    labels = jnp.zeros((tok * heads,), jnp.int32).at[position].set(target)
    arrived, places = (
        lax.all_to_all(outgoing, "seq", split_axis=0, concat_axis=0, tiled=True),
        lax.all_to_all(labels, "seq", split_axis=0, concat_axis=0, tiled=True),
    )
    tiles = jnp.zeros((pairs_dev * capacity, width), jnp.bfloat16).at[places].set(arrived)
    tiles = tiles.reshape(pairs_dev, capacity, width)
    pieces = []
    for index in range(3):
        start = index * block_rows
        stop = start + block_rows
        pieces.append(
            attend(
                tiles[:, start:stop, :head_size],
                tiles[:, :stop, head_size : 2 * head_size],
                tiles[:, :stop, 2 * head_size :],
                start,
                scale,
            )
        )
    results = jnp.concatenate(pieces, axis=1)
    flat_results = results.reshape(pairs_dev * capacity, head_size)
    replies = flat_results[places]
    returned = lax.all_to_all(replies, "seq", split_axis=0, concat_axis=0, tiled=True)
    return returned[position].reshape(tok, heads, head_size)


def partial_softmax(query, keys, values, lab_col, lab_row, scale, causal):
    rows, head_size = query.shape
    span = keys.shape[0]
    contract = (((1,), (1,)), ((), ()))
    scores = lax.dot_general(query, keys, contract, preferred_element_type=jnp.float32)
    same = lab_col == lab_row
    if causal:
        past = span - rows
        row_id = lax.broadcasted_iota(jnp.int32, (rows, rows), 0)
        col_id = lax.broadcasted_iota(jnp.int32, (rows, rows), 1)
        last = jnp.where(same[:, past:] & (col_id <= row_id), scores[:, past:], NEG)
        if past:
            first = jnp.where(same[:, :past], scores[:, :past], NEG)
            scores = jnp.concatenate([first, last], axis=1)
        else:
            scores = last
    else:
        scores = jnp.where(same, scores, NEG)
    factor = scale * math.log2(math.e)
    peak = jnp.max(scores, axis=1, keepdims=True) * factor
    expo = jnp.exp2(scores * factor - peak)
    total = jnp.sum(expo, axis=1, keepdims=True)
    out = jnp.dot(expo.astype(jnp.bfloat16), values, preferred_element_type=jnp.float32)
    return (out / total).astype(jnp.bfloat16), peak, total


def exchange_kernel(
    nseq, held, group, x_ref, lab_ref, out_ref, recv, qrecv, labs, obuf, sbuf, part, stats, merged, cols,
    x_send, x_recv, q_send, q_recv, l_send, l_recv, o_send, o_recv, s_send, s_recv,
    own_x, own_l, own_o, own_s, m_sem,
):
    me = lax.axis_index("seq")
    half = nseq // 2
    low = me < half
    up = me >= half
    side = me // half
    base = side * half
    mine = lax.rem(me, half)
    tok, width = x_ref.shape[1:]
    size = width // 3
    scale = 1.0 / math.sqrt(size)
    rows = group * tok

    def remote(src, dst, send, recv_sem, peer):
        return pltpu.make_async_remote_copy(
            src_ref=src, dst_ref=dst, send_sem=send, recv_sem=recv_sem,
            device_id={"seq": peer}, device_id_type=pl.DeviceIdType.MESH,
        )

    def x_copy(j, p):
        return remote(x_ref.at[p * held + j], recv.at[j, mine],
                      x_send.at[j, p], x_recv.at[j, mine], base + p)

    def x_arrival(j, p):
        return remote(x_ref.at[0], recv.at[j, p], x_send.at[j, p], x_recv.at[j, p], base + p)

    def q_copy(j, p):
        return remote(x_ref.at[p * held + j, :, pl.ds(0, size)], qrecv.at[j, mine],
                      q_send.at[j, p], q_recv.at[j, mine], p)

    def q_arrival(j, p):
        return remote(x_ref.at[0, :, pl.ds(0, size)], qrecv.at[j, p],
                      q_send.at[j, p], q_recv.at[j, p], half + p)

    def l_copy(peer):
        return remote(lab_ref.at[lax.rem(peer, half)], labs.at[me],
                      l_send.at[peer], l_recv.at[me], peer)

    def l_arrival(peer):
        return remote(lab_ref.at[0], labs.at[peer], l_send.at[peer], l_recv.at[peer], peer)

    def o_copy_low(j, p):
        return remote(obuf.at[j, p], out_ref.at[mine * held + j],
                      o_send.at[j, p], o_recv.at[0, j, mine], p)

    def o_arrival_low(j, p):
        return remote(obuf.at[j, 0], out_ref.at[p * held + j],
                      o_send.at[j, p], o_recv.at[0, j, p], p)

    def o_copy_up(j, peer):
        return remote(obuf.at[j, peer], part.at[side, mine * held + j],
                      o_send.at[j, peer], o_recv.at[side, j, mine], peer)

    def o_arrival_up(which, j, p):
        return remote(obuf.at[j, 0], part.at[which, p * held + j],
                      o_send.at[j, which * half + p], o_recv.at[which, j, p], which * half + p)

    def s_copy(j, peer):
        return remote(sbuf.at[j, peer], stats.at[side, mine, j],
                      s_send.at[j, peer], s_recv.at[side, j, mine], peer)

    def s_arrival(which, j, p):
        return remote(sbuf.at[j, 0], stats.at[which, p, j],
                      s_send.at[j, which * half + p], s_recv.at[which, j, p], which * half + p)

    def own_x_copy(j):
        return pltpu.make_async_copy(x_ref.at[mine * held + j], recv.at[j, mine], own_x.at[j])

    def own_o_low(j):
        return pltpu.make_async_copy(obuf.at[j, me], out_ref.at[mine * held + j], own_o.at[j])

    def own_o_up(j):
        return pltpu.make_async_copy(obuf.at[j, me], part.at[1, mine * held + j], own_o.at[j])

    def own_s_up(j):
        return pltpu.make_async_copy(sbuf.at[j, me], stats.at[1, mine, j], own_s.at[j])

    def result_copy(head):
        return pltpu.make_async_copy(merged.at[head], out_ref.at[head], m_sem.at[head])

    own_lab = pltpu.make_async_copy(lab_ref.at[mine], labs.at[me], own_l.at[0])

    def loop(start, stop, body):
        def step(k, carry):
            body(k)
            return carry

        lax.fori_loop(start, stop, step, 0)

    def each_peer(body):
        loop(1, nseq, lambda k: body(lax.rem(me + k, nseq)))

    def each_near(body):
        loop(1, half, lambda k: body(lax.rem(mine + k, half)))

    def each_far(body):
        loop(0, half, lambda k: body(lax.rem(mine + k, half)))

    own_lab.start()
    for j in range(held):
        own_x_copy(j).start()
    barrier = pltpu.get_barrier_semaphore()
    each_peer(lambda peer: pl.semaphore_signal(
        barrier, inc=1, device_id={"seq": peer}, device_id_type=pl.DeviceIdType.MESH))
    pl.semaphore_wait(barrier, nseq - 1)

    each_near(lambda p: l_copy(base + p).start())

    @pl.when(up)
    def _():
        each_far(lambda p: l_copy(p).start())

    def send_chunk(j):
        @pl.when(up)
        def _():
            each_far(lambda p: q_copy(j, p).start())

        each_near(lambda p: x_copy(j, p).start())

    loop(0, held, send_chunk)
    own_lab.wait()
    for j in range(held):
        own_x_copy(j).wait()
    each_near(lambda p: l_arrival(base + p).wait_recv())

    @pl.when(low)
    def _():
        each_far(lambda p: l_arrival(half + p).wait_recv())

    eye = lax.broadcasted_iota(jnp.int32, (tok, tok), 0) == lax.broadcasted_iota(
        jnp.int32, (tok, tok), 1)

    def to_col(line):
        return jnp.sum(jnp.where(eye, line, jnp.zeros_like(line)), axis=1, keepdims=True)

    def to_row(col):
        return jnp.sum(jnp.where(eye, col, jnp.zeros_like(col)), axis=0, keepdims=True)

    def keep(j, first, block, result, peak, total):
        for g in range(group):
            source = first + block * group + g
            obuf[j, source] = result[g * tok : (g + 1) * tok]
            sbuf[j, source, 0:1, :] = to_row(peak[g * tok : (g + 1) * tok])
            sbuf[j, source, 1:2, :] = to_row(total[g * tok : (g + 1) * tok])

    def chunk(j):
        def fill_cols(p):
            cols[base + p] = to_col(labs[base + p, pl.ds(j, 1), :])

        loop(0, half, fill_cols)

        @pl.when(low)
        def _():
            def fill_far(p):
                cols[half + p] = to_col(labs[half + p, pl.ds(j, 1), :])

            loop(0, half, fill_far)

        for block in range(half // group):
            for g in range(group):
                p = block * group + g

                @pl.when(mine != p)
                def _():
                    x_arrival(j, p).wait_recv()

            span = (block + 1) * group
            query = recv[j, block * group : span, :, :size].reshape(rows, size)
            keys = recv[j, :span, :, size : 2 * size].reshape(span * tok, size)
            values = recv[j, :span, :, 2 * size :].reshape(span * tok, size)
            lab_row = jnp.concatenate(
                [labs[base + p, pl.ds(j, 1), :] for p in range(span)], axis=1)
            lab_col = jnp.concatenate(
                [cols[base + block * group + g] for g in range(group)], axis=0)
            result, peak, total = partial_softmax(
                query, keys, values, lab_col, lab_row, scale, True)
            keep(j, base, block, result, peak, total)
            for g in range(group):
                p = block * group + g

                @pl.when(low & (mine != p))
                def _():
                    o_copy_low(j, p).start()

                @pl.when(low & (mine == p))
                def _():
                    own_o_low(j).start()

                @pl.when(up & (mine != p))
                def _():
                    o_copy_up(j, half + p).start()
                    s_copy(j, half + p).start()

                @pl.when(up & (mine == p))
                def _():
                    own_o_up(j).start()
                    own_s_up(j).start()

        @pl.when(low)
        def _():
            for block in range(half // group):
                for g in range(group):
                    q_arrival(j, block * group + g).wait_recv()
                query = qrecv[j, block * group : (block + 1) * group].reshape(rows, size)
                keys = recv[j, :, :, size : 2 * size].reshape(half * tok, size)
                values = recv[j, :, :, 2 * size :].reshape(half * tok, size)
                lab_row = jnp.concatenate(
                    [labs[p, pl.ds(j, 1), :] for p in range(half)], axis=1)
                lab_col = jnp.concatenate(
                    [cols[half + block * group + g] for g in range(group)], axis=0)
                result, peak, total = partial_softmax(
                    query, keys, values, lab_col, lab_row, scale, False)
                keep(j, half, block, result, peak, total)
                for g in range(group):
                    o_copy_up(j, half + block * group + g).start()
                    s_copy(j, half + block * group + g).start()

    loop(0, held, chunk)

    each_near(lambda p: l_copy(base + p).wait_send())
    loop(0, held, lambda j: each_near(lambda p: x_copy(j, p).wait_send()))

    @pl.when(low)
    def _():
        def finish(j):
            own_o_low(j).wait()

            def near(p):
                o_copy_low(j, p).wait_send()
                o_arrival_low(j, p).wait_recv()

            def far(p):
                o_copy_up(j, half + p).wait_send()
                s_copy(j, half + p).wait_send()

            each_near(near)
            each_far(far)

        loop(0, held, finish)

    @pl.when(up)
    def _():
        each_far(lambda p: l_copy(p).wait_send())
        loop(0, held, lambda j: each_far(lambda p: q_copy(j, p).wait_send()))

        def finish(j):
            own_o_up(j).wait()
            own_s_up(j).wait()

            def near(p):
                o_copy_up(j, half + p).wait_send()
                s_copy(j, half + p).wait_send()
                o_arrival_up(1, j, p).wait_recv()
                s_arrival(1, j, p).wait_recv()

            each_near(near)

            def merge(p):
                o_arrival_up(0, j, p).wait_recv()
                s_arrival(0, j, p).wait_recv()
                head = p * held + j
                peak0, peak1 = stats[0, p, j, 0:1, :], stats[1, p, j, 0:1, :]
                peak = jnp.maximum(peak0, peak1)
                weight0 = stats[0, p, j, 1:2, :] * jnp.exp2(peak0 - peak)
                weight1 = stats[1, p, j, 1:2, :] * jnp.exp2(peak1 - peak)
                total = weight0 + weight1
                merged[head] = (
                    to_col(weight0 / total) * part[0, head].astype(jnp.float32)
                    + to_col(weight1 / total) * part[1, head].astype(jnp.float32)
                ).astype(jnp.bfloat16)
                result_copy(head).start()

            loop(0, half, merge)

        loop(0, held, finish)
        loop(0, half * held, lambda head: result_copy(head).wait())


def by_head(qkv, routes):
    tok, heads, width = qkv.shape
    size = width // 3
    nseq = lax.axis_size("seq")
    half = nseq // 2
    held = heads // half
    group = 2 if half % 2 == 0 else 1
    lines = jnp.transpose(routes, (1, 0)).reshape(half, held, tok)
    lines = jnp.pad(lines, ((0, 0), (0, LABEL_ROWS - held), (0, 0)))
    dma = pltpu.SemaphoreType.DMA
    out = pl.pallas_call(
        functools.partial(exchange_kernel, nseq, held, group),
        out_shape=jax.ShapeDtypeStruct((heads, tok, size), jnp.bfloat16),
        in_specs=[pl.BlockSpec(memory_space=pl.ANY)] * 2,
        out_specs=pl.BlockSpec(memory_space=pl.ANY),
        scratch_shapes=[
            pltpu.VMEM((held, half, tok, width), jnp.bfloat16),
            pltpu.VMEM((held, half, tok, size), jnp.bfloat16),
            pltpu.VMEM((nseq, LABEL_ROWS, tok), jnp.int32),
            pltpu.VMEM((held, nseq, tok, size), jnp.bfloat16),
            pltpu.VMEM((held, nseq, 8, tok), jnp.float32),
            pltpu.VMEM((2, heads, tok, size), jnp.bfloat16),
            pltpu.VMEM((2, half, held, 8, tok), jnp.float32),
            pltpu.VMEM((heads, tok, size), jnp.bfloat16),
            pltpu.VMEM((nseq, tok, 1), jnp.int32),
            dma((held, half)),
            dma((held, half)),
            dma((held, half)),
            dma((held, half)),
            dma((nseq,)),
            dma((nseq,)),
            dma((held, nseq)),
            dma((2, held, half)),
            dma((held, nseq)),
            dma((2, held, half)),
            dma((held,)),
            dma((1,)),
            dma((held,)),
            dma((held,)),
            dma((heads,)),
        ],
        compiler_params=pltpu.CompilerParams(
            collective_id=0, has_side_effects=True, vmem_limit_bytes=48 * 2**20
        ),
        name="exchange",
    )(jnp.transpose(qkv, (1, 0, 2)), lines)
    return jnp.transpose(out, (1, 0, 2))


def solution(mesh):
    placed = (P(("groups", "seq"), None, None), P(("groups", "seq"), None))
    nseq = mesh.shape["seq"]

    def local(qkv, routes):
        heads = qkv.shape[1]
        half = nseq // 2
        if nseq % 2 == 0 and heads % half == 0 and heads // half <= LABEL_ROWS:
            return by_head(qkv, routes)
        return routed(qkv, routes)

    return jax.shard_map(
        local,
        mesh=mesh,
        in_specs=placed,
        out_specs=P(("groups", "seq"), None, None),
        check_vma=False,
    )
```

```python
import functools
import math

import jax
import jax.numpy as jnp
from jax import lax
from jax.experimental import pallas as pl
from jax.experimental.pallas import tpu as pltpu
from jax.sharding import PartitionSpec as P

CLEN = 1024
LABEL_ROWS = 8
NEG = -1e36


def entering(part, axis, combine, identity):
    place = lax.axis_index(axis)
    gathered = lax.all_gather(part, axis)
    state = jnp.zeros_like(part) + jnp.asarray(identity, part.dtype)

    def one(turn, state):
        return combine(state, lax.dynamic_index_in_dim(gathered, turn, 0, False))

    return lax.fori_loop(0, place, one, state)


def attend(queries, keys, values, start, scale):
    block_rows = queries.shape[1]
    span = keys.shape[1]
    scores = jnp.einsum("pqd,pkd->pqk", queries, keys, preferred_element_type=jnp.float32) * scale
    rows = start + jnp.arange(block_rows, dtype=jnp.int32)[:, None]
    cols = jnp.arange(span, dtype=jnp.int32)[None, :]
    scores = jnp.where((cols <= rows)[None], scores, -1e30)
    peak = jnp.max(scores, axis=2, keepdims=True)
    expo = jnp.exp(scores - peak)
    weights = (expo / jnp.sum(expo, axis=2, keepdims=True)).astype(jnp.bfloat16)
    return jnp.einsum("pqk,pkd->pqd", weights, values, preferred_element_type=jnp.float32).astype(
        jnp.bfloat16
    )


def routed(qkv, routes):
    tok, heads, width = qkv.shape
    head_size = width // 3
    nseq = lax.axis_size("seq")
    clusters = nseq * tok // CLEN
    pairs_dev = heads * tok // CLEN
    capacity = 3 * CLEN // 2
    block_rows = CLEN // 2
    share = CLEN // nseq
    rows_peer = pairs_dev * share
    total_pairs = heads * clusters
    scale = 1.0 / math.sqrt(head_size)
    member = routes[:, :, None] == jnp.arange(clusters, dtype=jnp.int32)[None, None, :]
    member_flat = member.reshape(tok, total_pairs)
    counts = jnp.sum(member_flat.astype(jnp.int32), axis=0)
    earlier = (jnp.arange(tok)[:, None] > jnp.arange(tok)[None, :]).astype(jnp.bfloat16)
    before = jnp.dot(earlier, member_flat.astype(jnp.bfloat16), preferred_element_type=jnp.float32)
    rank = jnp.sum(jnp.where(member, before.reshape(tok, heads, clusters), 0.0), axis=2).astype(
        jnp.int32
    )
    prefix = entering(counts, "seq", lambda first, second: first + second, jnp.zeros_like(counts))

    def lookup(table):
        return jnp.sum(jnp.where(member, table.reshape(heads, clusters)[None], 0), axis=2)

    group_counts = counts.reshape(total_pairs // pairs_dev, pairs_dev)
    within = (jnp.cumsum(group_counts, axis=1) - group_counts).reshape(total_pairs)
    slot = lookup(prefix) + rank
    pair_index = jnp.arange(heads, dtype=jnp.int32)[None, :] * clusters + routes
    owner = pair_index // pairs_dev
    local_pair = pair_index % pairs_dev
    position = (owner * rows_peer + lookup(within) + rank).reshape(tok * heads)
    target = (local_pair * capacity + slot).reshape(tok * heads)
    outgoing = (
        jnp.zeros((tok * heads, width), jnp.bfloat16)
        .at[position]
        .set(qkv.reshape(tok * heads, width))
    )
    labels = jnp.zeros((tok * heads,), jnp.int32).at[position].set(target)
    arrived, places = (
        lax.all_to_all(outgoing, "seq", split_axis=0, concat_axis=0, tiled=True),
        lax.all_to_all(labels, "seq", split_axis=0, concat_axis=0, tiled=True),
    )
    tiles = jnp.zeros((pairs_dev * capacity, width), jnp.bfloat16).at[places].set(arrived)
    tiles = tiles.reshape(pairs_dev, capacity, width)
    pieces = []
    for index in range(3):
        start = index * block_rows
        stop = start + block_rows
        pieces.append(
            attend(
                tiles[:, start:stop, :head_size],
                tiles[:, :stop, head_size : 2 * head_size],
                tiles[:, :stop, 2 * head_size :],
                start,
                scale,
            )
        )
    results = jnp.concatenate(pieces, axis=1)
    flat_results = results.reshape(pairs_dev * capacity, head_size)
    replies = flat_results[places]
    returned = lax.all_to_all(replies, "seq", split_axis=0, concat_axis=0, tiled=True)
    return returned[position].reshape(tok, heads, head_size)


def partial_softmax(query, keys, values, scale, causal):
    rows = query.shape[0]
    span = keys.shape[0]
    size = values.shape[1] // 2
    contract = (((1,), (1,)), ((), ()))
    scores = lax.dot_general(query, keys, contract, preferred_element_type=jnp.float32)
    if causal:
        past = span - rows
        row_id = lax.broadcasted_iota(jnp.int32, (rows, rows), 0)
        col_id = lax.broadcasted_iota(jnp.int32, (rows, rows), 1)
        last = jnp.where(col_id <= row_id, scores[:, past:], NEG)
        scores = jnp.concatenate([scores[:, :past], last], axis=1) if past else last
    factor = scale * math.log2(math.e)
    peak = jnp.max(scores, axis=1, keepdims=True) * factor
    expo = jnp.exp2(scores * factor - peak).astype(jnp.bfloat16)
    out = jnp.dot(expo, values, preferred_element_type=jnp.float32)
    total = out[:, size:]
    return (out[:, :size] / total).astype(jnp.bfloat16), peak, total[:, :1]


def exchange_kernel(
    nseq, held, group, x_ref, lab_ref, out_ref, recv, qrecv, labs, obuf, sbuf, part, stats, merged, hot, cold,
    x_send, x_recv, q_send, q_recv, l_send, l_recv, o_send, o_recv, s_send, s_recv,
    own_x, own_l, own_o, own_s, m_sem,
):
    me = lax.axis_index("seq")
    half = nseq // 2
    low = me < half
    up = me >= half
    side = me // half
    base = side * half
    mine = lax.rem(me, half)
    tok, width = x_ref.shape[1:]
    size = width // 3
    scale = 1.0 / math.sqrt(size)
    rows = group * tok
    wide = 2 * group if half % (2 * group) == 0 else group

    def remote(src, dst, send, recv_sem, peer):
        return pltpu.make_async_remote_copy(
            src_ref=src, dst_ref=dst, send_sem=send, recv_sem=recv_sem,
            device_id={"seq": peer}, device_id_type=pl.DeviceIdType.MESH,
        )

    def x_copy(j, p):
        return remote(x_ref.at[p * held + j], recv.at[j, mine],
                      x_send.at[j, p], x_recv.at[j, mine], base + p)

    def x_arrival(j, p):
        return remote(x_ref.at[0], recv.at[j, p], x_send.at[j, p], x_recv.at[j, p], base + p)

    def q_copy(j, p):
        return remote(x_ref.at[p * held + j, :, pl.ds(0, size)], qrecv.at[j, mine],
                      q_send.at[j, p], q_recv.at[j, mine], p)

    def q_arrival(j, p):
        return remote(x_ref.at[0, :, pl.ds(0, size)], qrecv.at[j, p],
                      q_send.at[j, p], q_recv.at[j, p], half + p)

    def l_copy(peer):
        return remote(lab_ref.at[lax.rem(peer, half)], labs.at[me],
                      l_send.at[peer], l_recv.at[me], peer)

    def l_arrival(peer):
        return remote(lab_ref.at[0], labs.at[peer], l_send.at[peer], l_recv.at[peer], peer)

    def o_copy_low(j, p):
        return remote(obuf.at[j, p], out_ref.at[mine * held + j],
                      o_send.at[j, p], o_recv.at[0, j, mine], p)

    def o_arrival_low(j, p):
        return remote(obuf.at[j, 0], out_ref.at[p * held + j],
                      o_send.at[j, p], o_recv.at[0, j, p], p)

    def o_copy_up(j, peer):
        return remote(obuf.at[j, peer], part.at[side, mine * held + j],
                      o_send.at[j, peer], o_recv.at[side, j, mine], peer)

    def o_arrival_up(which, j, p):
        return remote(obuf.at[j, 0], part.at[which, p * held + j],
                      o_send.at[j, which * half + p], o_recv.at[which, j, p], which * half + p)

    def s_copy(j, peer):
        return remote(sbuf.at[j, peer], stats.at[side, mine, j],
                      s_send.at[j, peer], s_recv.at[side, j, mine], peer)

    def s_arrival(which, j, p):
        return remote(sbuf.at[j, 0], stats.at[which, p, j],
                      s_send.at[j, which * half + p], s_recv.at[which, j, p], which * half + p)

    def own_x_copy(j):
        return pltpu.make_async_copy(x_ref.at[mine * held + j], recv.at[j, mine], own_x.at[j])

    def own_o_low(j):
        return pltpu.make_async_copy(obuf.at[j, me], out_ref.at[mine * held + j], own_o.at[j])

    def own_o_up(j):
        return pltpu.make_async_copy(obuf.at[j, me], part.at[1, mine * held + j], own_o.at[j])

    def own_s_up(j):
        return pltpu.make_async_copy(sbuf.at[j, me], stats.at[1, mine, j], own_s.at[j])

    def result_copy(head):
        return pltpu.make_async_copy(merged.at[head], out_ref.at[head], m_sem.at[head])

    own_lab = pltpu.make_async_copy(lab_ref.at[mine], labs.at[me], own_l.at[0])

    def loop(start, stop, body):
        def step(k, carry):
            body(k)
            return carry

        lax.fori_loop(start, stop, step, 0)

    def each_peer(body):
        loop(1, nseq, lambda k: body(lax.rem(me + k, nseq)))

    def each_near(body):
        loop(1, half, lambda k: body(lax.rem(mine + k, half)))

    def each_far(body):
        loop(0, half, lambda k: body(lax.rem(mine + k, half)))

    own_lab.start()
    for j in range(held):
        own_x_copy(j).start()
    barrier = pltpu.get_barrier_semaphore()
    each_peer(lambda peer: pl.semaphore_signal(
        barrier, inc=1, device_id={"seq": peer}, device_id_type=pl.DeviceIdType.MESH))
    pl.semaphore_wait(barrier, nseq - 1)

    each_near(lambda p: l_copy(base + p).start())

    @pl.when(up)
    def _():
        each_far(lambda p: l_copy(p).start())

    def send_chunk(j):
        @pl.when(up)
        def _():
            each_far(lambda p: q_copy(j, p).start())

        each_near(lambda p: x_copy(j, p).start())

    loop(0, held, send_chunk)
    own_lab.wait()
    for j in range(held):
        own_x_copy(j).wait()
    each_near(lambda p: l_arrival(base + p).wait_recv())

    @pl.when(low)
    def _():
        each_far(lambda p: l_arrival(half + p).wait_recv())

    eye = lax.broadcasted_iota(jnp.int32, (tok, tok), 0) == lax.broadcasted_iota(
        jnp.int32, (tok, tok), 1)

    def to_col(line):
        return jnp.sum(jnp.where(eye, line, jnp.zeros_like(line)), axis=1, keepdims=True)

    def to_row(col):
        return jnp.sum(jnp.where(eye, col, jnp.zeros_like(col)), axis=0, keepdims=True)

    def keep(j, first, count, result, peak, total):
        for g in range(count):
            part_rows = slice(g * tok, (g + 1) * tok)
            obuf[j, first + g] = result[part_rows]
            sbuf[j, first + g, 0:1, :] = to_row(peak[part_rows])
            sbuf[j, first + g, 1:2, :] = to_row(total[part_rows])

    def chunk(j):
        def label_match(source):
            col = to_col(labs[source, pl.ds(j, 1), :])
            return lax.broadcasted_iota(jnp.int32, (tok, size), 1) == col

        def fill_near(p):
            match = label_match(base + p)
            hot[base + p] = jnp.where(match, 1.0, 0.0).astype(jnp.bfloat16)
            cold[p] = jnp.where(match, 0.0, NEG).astype(jnp.bfloat16)

        loop(0, half, fill_near)
        each_near(lambda p: x_arrival(j, p).wait_recv())

        def keys_of(span):
            keys = recv[j, :span, :, size : 2 * size].reshape(span * tok, size)
            return jnp.concatenate([keys, cold[:span].reshape(span * tok, size)], axis=1)

        def values_of(span):
            values = recv[j, :span, :, 2 * size :].reshape(span * tok, size)
            return jnp.concatenate([values, jnp.ones((span * tok, size), jnp.bfloat16)], axis=1)

        @pl.when(low)
        def _():
            def fill_far(p):
                hot[half + p] = jnp.where(label_match(half + p), 1.0, 0.0).astype(jnp.bfloat16)

            loop(0, half, fill_far)
            each_far(lambda p: q_arrival(j, p).wait_recv())
            for first in range(0, half, wide):
                query = jnp.concatenate([
                    qrecv[j, first : first + wide].reshape(wide * tok, size),
                    hot[half + first : half + first + wide].reshape(wide * tok, size)], axis=1)
                result, peak, total = partial_softmax(
                    query, keys_of(half), values_of(half), scale, False)
                keep(j, half + first, wide, result, peak, total)
                for g in range(wide):
                    o_copy_up(j, half + first + g).start()
                    s_copy(j, half + first + g).start()

        for first in range(0, half, group):
            query = jnp.concatenate([
                recv[j, first : first + group, :, :size].reshape(rows, size),
                hot[pl.ds(base + first, group)].reshape(rows, size)], axis=1)
            result, peak, total = partial_softmax(
                query, keys_of(first + group), values_of(first + group), scale, True)
            keep(j, base + first, group, result, peak, total)

        @pl.when(low)
        def _():
            each_near(lambda p: o_copy_low(j, p).start())
            own_o_low(j).start()

        @pl.when(up)
        def _():
            def send_up(p):
                o_copy_up(j, half + p).start()
                s_copy(j, half + p).start()

            each_near(send_up)
            own_o_up(j).start()
            own_s_up(j).start()

    loop(0, held, chunk)

    each_near(lambda p: l_copy(base + p).wait_send())
    loop(0, held, lambda j: each_near(lambda p: x_copy(j, p).wait_send()))

    @pl.when(low)
    def _():
        def finish(j):
            own_o_low(j).wait()

            def near(p):
                o_copy_low(j, p).wait_send()
                o_arrival_low(j, p).wait_recv()

            def far(p):
                o_copy_up(j, half + p).wait_send()
                s_copy(j, half + p).wait_send()

            each_near(near)
            each_far(far)

        loop(0, held, finish)

    @pl.when(up)
    def _():
        each_far(lambda p: l_copy(p).wait_send())
        loop(0, held, lambda j: each_far(lambda p: q_copy(j, p).wait_send()))

        def finish(j):
            own_o_up(j).wait()
            own_s_up(j).wait()

            def near(p):
                o_copy_up(j, half + p).wait_send()
                s_copy(j, half + p).wait_send()
                o_arrival_up(1, j, p).wait_recv()
                s_arrival(1, j, p).wait_recv()

            each_near(near)

            def merge(p):
                o_arrival_up(0, j, p).wait_recv()
                s_arrival(0, j, p).wait_recv()
                head = p * held + j
                peak0, peak1 = stats[0, p, j, 0:1, :], stats[1, p, j, 0:1, :]
                peak = jnp.maximum(peak0, peak1)
                weight0 = stats[0, p, j, 1:2, :] * jnp.exp2(peak0 - peak)
                weight1 = stats[1, p, j, 1:2, :] * jnp.exp2(peak1 - peak)
                total = weight0 + weight1
                merged[head] = (
                    to_col(weight0 / total) * part[0, head].astype(jnp.float32)
                    + to_col(weight1 / total) * part[1, head].astype(jnp.float32)
                ).astype(jnp.bfloat16)
                result_copy(head).start()

            loop(0, half, merge)

        loop(0, held, finish)
        loop(0, half * held, lambda head: result_copy(head).wait())


def by_head(qkv, routes):
    tok, heads, width = qkv.shape
    size = width // 3
    nseq = lax.axis_size("seq")
    half = nseq // 2
    held = heads // half
    group = 2 if half % 2 == 0 else 1
    lines = jnp.transpose(routes, (1, 0)).reshape(half, held, tok)
    lines = jnp.pad(lines, ((0, 0), (0, LABEL_ROWS - held), (0, 0)))
    dma = pltpu.SemaphoreType.DMA
    out = pl.pallas_call(
        functools.partial(exchange_kernel, nseq, held, group),
        out_shape=jax.ShapeDtypeStruct((heads, tok, size), jnp.bfloat16),
        in_specs=[pl.BlockSpec(memory_space=pl.ANY)] * 2,
        out_specs=pl.BlockSpec(memory_space=pl.ANY),
        scratch_shapes=[
            pltpu.VMEM((held, half, tok, width), jnp.bfloat16),
            pltpu.VMEM((held, half, tok, size), jnp.bfloat16),
            pltpu.VMEM((nseq, LABEL_ROWS, tok), jnp.int32),
            pltpu.VMEM((held, nseq, tok, size), jnp.bfloat16),
            pltpu.VMEM((held, nseq, 8, tok), jnp.float32),
            pltpu.VMEM((2, heads, tok, size), jnp.bfloat16),
            pltpu.VMEM((2, half, held, 8, tok), jnp.float32),
            pltpu.VMEM((heads, tok, size), jnp.bfloat16),
            pltpu.VMEM((nseq, tok, size), jnp.bfloat16),
            pltpu.VMEM((half, tok, size), jnp.bfloat16),
            dma((held, half)),
            dma((held, half)),
            dma((held, half)),
            dma((held, half)),
            dma((nseq,)),
            dma((nseq,)),
            dma((held, nseq)),
            dma((2, held, half)),
            dma((held, nseq)),
            dma((2, held, half)),
            dma((held,)),
            dma((1,)),
            dma((held,)),
            dma((held,)),
            dma((heads,)),
        ],
        compiler_params=pltpu.CompilerParams(
            collective_id=0, has_side_effects=True, vmem_limit_bytes=48 * 2**20
        ),
        name="exchange",
    )(jnp.transpose(qkv, (1, 0, 2)), lines)
    return jnp.transpose(out, (1, 0, 2))


def solution(mesh):
    placed = (P(("groups", "seq"), None, None), P(("groups", "seq"), None))
    nseq = mesh.shape["seq"]

    def local(qkv, routes):
        heads = qkv.shape[1]
        half = nseq // 2
        clusters = nseq * qkv.shape[0] // CLEN
        fits = clusters <= qkv.shape[2] // 3
        if fits and nseq % 2 == 0 and heads % half == 0 and heads // half <= LABEL_ROWS:
            return by_head(qkv, routes)
        return routed(qkv, routes)

    return jax.shard_map(
        local,
        mesh=mesh,
        in_specs=placed,
        out_specs=P(("groups", "seq"), None, None),
        check_vma=False,
    )
```

```python
import functools
import math

import jax
import jax.numpy as jnp
from jax import lax
from jax.experimental import pallas as pl
from jax.experimental.pallas import tpu as pltpu
from jax.sharding import PartitionSpec as P

CLEN = 1024
LABEL_ROWS = 8
NEG = -1e36


def entering(part, axis, combine, identity):
    place = lax.axis_index(axis)
    gathered = lax.all_gather(part, axis)
    state = jnp.zeros_like(part) + jnp.asarray(identity, part.dtype)

    def one(turn, state):
        return combine(state, lax.dynamic_index_in_dim(gathered, turn, 0, False))

    return lax.fori_loop(0, place, one, state)


def attend(queries, keys, values, start, scale):
    block_rows = queries.shape[1]
    span = keys.shape[1]
    scores = jnp.einsum("pqd,pkd->pqk", queries, keys, preferred_element_type=jnp.float32) * scale
    rows = start + jnp.arange(block_rows, dtype=jnp.int32)[:, None]
    cols = jnp.arange(span, dtype=jnp.int32)[None, :]
    scores = jnp.where((cols <= rows)[None], scores, -1e30)
    peak = jnp.max(scores, axis=2, keepdims=True)
    expo = jnp.exp(scores - peak)
    weights = (expo / jnp.sum(expo, axis=2, keepdims=True)).astype(jnp.bfloat16)
    return jnp.einsum("pqk,pkd->pqd", weights, values, preferred_element_type=jnp.float32).astype(
        jnp.bfloat16
    )


def routed(qkv, routes):
    tok, heads, width = qkv.shape
    head_size = width // 3
    nseq = lax.axis_size("seq")
    clusters = nseq * tok // CLEN
    pairs_dev = heads * tok // CLEN
    capacity = 3 * CLEN // 2
    block_rows = CLEN // 2
    share = CLEN // nseq
    rows_peer = pairs_dev * share
    total_pairs = heads * clusters
    scale = 1.0 / math.sqrt(head_size)
    member = routes[:, :, None] == jnp.arange(clusters, dtype=jnp.int32)[None, None, :]
    member_flat = member.reshape(tok, total_pairs)
    counts = jnp.sum(member_flat.astype(jnp.int32), axis=0)
    earlier = (jnp.arange(tok)[:, None] > jnp.arange(tok)[None, :]).astype(jnp.bfloat16)
    before = jnp.dot(earlier, member_flat.astype(jnp.bfloat16), preferred_element_type=jnp.float32)
    rank = jnp.sum(jnp.where(member, before.reshape(tok, heads, clusters), 0.0), axis=2).astype(
        jnp.int32
    )
    prefix = entering(counts, "seq", lambda first, second: first + second, jnp.zeros_like(counts))

    def lookup(table):
        return jnp.sum(jnp.where(member, table.reshape(heads, clusters)[None], 0), axis=2)

    group_counts = counts.reshape(total_pairs // pairs_dev, pairs_dev)
    within = (jnp.cumsum(group_counts, axis=1) - group_counts).reshape(total_pairs)
    slot = lookup(prefix) + rank
    pair_index = jnp.arange(heads, dtype=jnp.int32)[None, :] * clusters + routes
    owner = pair_index // pairs_dev
    local_pair = pair_index % pairs_dev
    position = (owner * rows_peer + lookup(within) + rank).reshape(tok * heads)
    target = (local_pair * capacity + slot).reshape(tok * heads)
    outgoing = (
        jnp.zeros((tok * heads, width), jnp.bfloat16)
        .at[position]
        .set(qkv.reshape(tok * heads, width))
    )
    labels = jnp.zeros((tok * heads,), jnp.int32).at[position].set(target)
    arrived, places = (
        lax.all_to_all(outgoing, "seq", split_axis=0, concat_axis=0, tiled=True),
        lax.all_to_all(labels, "seq", split_axis=0, concat_axis=0, tiled=True),
    )
    tiles = jnp.zeros((pairs_dev * capacity, width), jnp.bfloat16).at[places].set(arrived)
    tiles = tiles.reshape(pairs_dev, capacity, width)
    pieces = []
    for index in range(3):
        start = index * block_rows
        stop = start + block_rows
        pieces.append(
            attend(
                tiles[:, start:stop, :head_size],
                tiles[:, :stop, head_size : 2 * head_size],
                tiles[:, :stop, 2 * head_size :],
                start,
                scale,
            )
        )
    results = jnp.concatenate(pieces, axis=1)
    flat_results = results.reshape(pairs_dev * capacity, head_size)
    replies = flat_results[places]
    returned = lax.all_to_all(replies, "seq", split_axis=0, concat_axis=0, tiled=True)
    return returned[position].reshape(tok, heads, head_size)


def partial_softmax(query, keys, values, scale, causal):
    rows = query.shape[0]
    span = keys.shape[0]
    size = values.shape[1] // 2
    contract = (((1,), (1,)), ((), ()))
    scores = lax.dot_general(query, keys, contract, preferred_element_type=jnp.float32)
    if causal:
        past = span - rows
        row_id = lax.broadcasted_iota(jnp.int32, (rows, rows), 0)
        col_id = lax.broadcasted_iota(jnp.int32, (rows, rows), 1)
        last = jnp.where(col_id <= row_id, scores[:, past:], NEG)
        scores = jnp.concatenate([scores[:, :past], last], axis=1) if past else last
    factor = scale * math.log2(math.e)
    peak = jnp.max(scores, axis=1, keepdims=True) * factor
    expo = jnp.exp2(scores * factor - peak).astype(jnp.bfloat16)
    out = jnp.dot(expo, values, preferred_element_type=jnp.float32)
    total = out[:, size:]
    return (out[:, :size] / total).astype(jnp.bfloat16), peak, total[:, :1]


def exchange_kernel(
    nseq, held, group, x_ref, lab_ref, out_ref, recv, qrecv, labs, obuf, sbuf, part, stats, merged, hot, cold,
    x_send, x_recv, q_send, q_recv, l_send, l_recv, o_send, o_recv, s_send, s_recv,
    own_x, own_l, own_o, own_s, m_sem,
):
    me = lax.axis_index("seq")
    half = nseq // 2
    low = me < half
    up = me >= half
    side = me // half
    base = side * half
    mine = lax.rem(me, half)
    tok, width = x_ref.shape[1:]
    size = width // 3
    scale = 1.0 / math.sqrt(size)
    rows = group * tok
    ahead = 2
    wide = 2 * group if half % (2 * group) == 0 else group

    def remote(src, dst, send, recv_sem, peer):
        return pltpu.make_async_remote_copy(
            src_ref=src, dst_ref=dst, send_sem=send, recv_sem=recv_sem,
            device_id={"seq": peer}, device_id_type=pl.DeviceIdType.MESH,
        )

    def x_copy(j, p):
        return remote(x_ref.at[p * held + j], recv.at[j, mine],
                      x_send.at[j, p], x_recv.at[j, mine], base + p)

    def x_arrival(j, p):
        return remote(x_ref.at[0], recv.at[j, p], x_send.at[j, p], x_recv.at[j, p], base + p)

    def q_copy(j, p):
        return remote(x_ref.at[p * held + j, :, pl.ds(0, size)], qrecv.at[j, mine],
                      q_send.at[j, p], q_recv.at[j, mine], p)

    def q_arrival(j, p):
        return remote(x_ref.at[0, :, pl.ds(0, size)], qrecv.at[j, p],
                      q_send.at[j, p], q_recv.at[j, p], half + p)

    def l_copy(peer):
        return remote(lab_ref.at[lax.rem(peer, half)], labs.at[me],
                      l_send.at[peer], l_recv.at[me], peer)

    def l_arrival(peer):
        return remote(lab_ref.at[0], labs.at[peer], l_send.at[peer], l_recv.at[peer], peer)

    def o_copy_low(j, p):
        return remote(obuf.at[j, p], out_ref.at[mine * held + j],
                      o_send.at[j, p], o_recv.at[0, j, mine], p)

    def o_arrival_low(j, p):
        return remote(obuf.at[j, 0], out_ref.at[p * held + j],
                      o_send.at[j, p], o_recv.at[0, j, p], p)

    def o_copy_up(j, peer):
        return remote(obuf.at[j, peer], part.at[side, mine * held + j],
                      o_send.at[j, peer], o_recv.at[side, j, mine], peer)

    def o_arrival_up(which, j, p):
        return remote(obuf.at[j, 0], part.at[which, p * held + j],
                      o_send.at[j, which * half + p], o_recv.at[which, j, p], which * half + p)

    def s_copy(j, peer):
        return remote(sbuf.at[j, peer], stats.at[side, mine, j],
                      s_send.at[j, peer], s_recv.at[side, j, mine], peer)

    def s_arrival(which, j, p):
        return remote(sbuf.at[j, 0], stats.at[which, p, j],
                      s_send.at[j, which * half + p], s_recv.at[which, j, p], which * half + p)

    def own_x_copy(j):
        return pltpu.make_async_copy(x_ref.at[mine * held + j], recv.at[j, mine], own_x.at[j])

    def own_o_low(j):
        return pltpu.make_async_copy(obuf.at[j, me], out_ref.at[mine * held + j], own_o.at[j])

    def own_o_up(j):
        return pltpu.make_async_copy(obuf.at[j, me], part.at[1, mine * held + j], own_o.at[j])

    def own_s_up(j):
        return pltpu.make_async_copy(sbuf.at[j, me], stats.at[1, mine, j], own_s.at[j])

    def result_copy(head):
        return pltpu.make_async_copy(merged.at[head], out_ref.at[head], m_sem.at[head])

    own_lab = pltpu.make_async_copy(lab_ref.at[mine], labs.at[me], own_l.at[0])

    def loop(start, stop, body):
        def step(k, carry):
            body(k)
            return carry

        lax.fori_loop(start, stop, step, 0)

    def each_peer(body):
        loop(1, nseq, lambda k: body(lax.rem(me + k, nseq)))

    def each_near(body):
        loop(1, half, lambda k: body(lax.rem(mine + k, half)))

    def each_far(body):
        loop(0, half, lambda k: body(lax.rem(mine + k, half)))

    own_lab.start()
    for j in range(held):
        own_x_copy(j).start()
    barrier = pltpu.get_barrier_semaphore()
    each_peer(lambda peer: pl.semaphore_signal(
        barrier, inc=1, device_id={"seq": peer}, device_id_type=pl.DeviceIdType.MESH))
    pl.semaphore_wait(barrier, nseq - 1)

    each_near(lambda p: l_copy(base + p).start())

    @pl.when(up)
    def _():
        each_far(lambda p: l_copy(p).start())

    def send_chunk(j):
        @pl.when(up)
        def _():
            each_far(lambda p: q_copy(j, p).start())

        each_near(lambda p: x_copy(j, p).start())

    loop(0, min(ahead, held), send_chunk)
    own_lab.wait()
    for j in range(held):
        own_x_copy(j).wait()
    each_near(lambda p: l_arrival(base + p).wait_recv())

    @pl.when(low)
    def _():
        each_far(lambda p: l_arrival(half + p).wait_recv())

    eye = lax.broadcasted_iota(jnp.int32, (tok, tok), 0) == lax.broadcasted_iota(
        jnp.int32, (tok, tok), 1)

    def to_col(line):
        return jnp.sum(jnp.where(eye, line, jnp.zeros_like(line)), axis=1, keepdims=True)

    def to_row(col):
        return jnp.sum(jnp.where(eye, col, jnp.zeros_like(col)), axis=0, keepdims=True)

    def keep(j, first, count, result, peak, total):
        for g in range(count):
            part_rows = slice(g * tok, (g + 1) * tok)
            obuf[j, first + g] = result[part_rows]
            sbuf[j, first + g, 0:1, :] = to_row(peak[part_rows])
            sbuf[j, first + g, 1:2, :] = to_row(total[part_rows])

    def chunk(j):
        def label_match(source):
            col = to_col(labs[source, pl.ds(j, 1), :])
            return lax.broadcasted_iota(jnp.int32, (tok, size), 1) == col

        def fill_near(p):
            match = label_match(base + p)
            hot[base + p] = jnp.where(match, 1.0, 0.0).astype(jnp.bfloat16)
            cold[p] = jnp.where(match, 0.0, NEG).astype(jnp.bfloat16)

        loop(0, half, fill_near)
        each_near(lambda p: x_arrival(j, p).wait_recv())

        @pl.when(low)
        def _():
            each_far(lambda p: q_arrival(j, p).wait_recv())

        @pl.when(j + ahead < held)
        def _():
            send_chunk(j + ahead)

        def keys_of(span):
            keys = recv[j, :span, :, size : 2 * size].reshape(span * tok, size)
            return jnp.concatenate([keys, cold[:span].reshape(span * tok, size)], axis=1)

        def values_of(span):
            values = recv[j, :span, :, 2 * size :].reshape(span * tok, size)
            return jnp.concatenate([values, jnp.ones((span * tok, size), jnp.bfloat16)], axis=1)

        @pl.when(low)
        def _():
            def fill_far(p):
                hot[half + p] = jnp.where(label_match(half + p), 1.0, 0.0).astype(jnp.bfloat16)

            loop(0, half, fill_far)
            for first in range(0, half, wide):
                query = jnp.concatenate([
                    qrecv[j, first : first + wide].reshape(wide * tok, size),
                    hot[half + first : half + first + wide].reshape(wide * tok, size)], axis=1)
                result, peak, total = partial_softmax(
                    query, keys_of(half), values_of(half), scale, False)
                keep(j, half + first, wide, result, peak, total)
                for g in range(wide):
                    o_copy_up(j, half + first + g).start()
                    s_copy(j, half + first + g).start()

        for first in range(0, half, group):
            query = jnp.concatenate([
                recv[j, first : first + group, :, :size].reshape(rows, size),
                hot[pl.ds(base + first, group)].reshape(rows, size)], axis=1)
            result, peak, total = partial_softmax(
                query, keys_of(first + group), values_of(first + group), scale, True)
            keep(j, base + first, group, result, peak, total)

        @pl.when(low)
        def _():
            each_near(lambda p: o_copy_low(j, p).start())
            own_o_low(j).start()

        @pl.when(up)
        def _():
            def send_up(p):
                o_copy_up(j, half + p).start()
                s_copy(j, half + p).start()

            each_near(send_up)
            own_o_up(j).start()
            own_s_up(j).start()

    loop(0, held, chunk)

    each_near(lambda p: l_copy(base + p).wait_send())
    loop(0, held, lambda j: each_near(lambda p: x_copy(j, p).wait_send()))

    @pl.when(low)
    def _():
        def finish(j):
            own_o_low(j).wait()

            def near(p):
                o_copy_low(j, p).wait_send()
                o_arrival_low(j, p).wait_recv()

            def far(p):
                o_copy_up(j, half + p).wait_send()
                s_copy(j, half + p).wait_send()

            each_near(near)
            each_far(far)

        loop(0, held, finish)

    @pl.when(up)
    def _():
        each_far(lambda p: l_copy(p).wait_send())
        loop(0, held, lambda j: each_far(lambda p: q_copy(j, p).wait_send()))

        def finish(j):
            own_o_up(j).wait()
            own_s_up(j).wait()

            def near(p):
                o_copy_up(j, half + p).wait_send()
                s_copy(j, half + p).wait_send()
                o_arrival_up(1, j, p).wait_recv()
                s_arrival(1, j, p).wait_recv()

            each_near(near)

            def merge(p):
                o_arrival_up(0, j, p).wait_recv()
                s_arrival(0, j, p).wait_recv()
                head = p * held + j
                peak0, peak1 = stats[0, p, j, 0:1, :], stats[1, p, j, 0:1, :]
                peak = jnp.maximum(peak0, peak1)
                weight0 = stats[0, p, j, 1:2, :] * jnp.exp2(peak0 - peak)
                weight1 = stats[1, p, j, 1:2, :] * jnp.exp2(peak1 - peak)
                total = weight0 + weight1
                merged[head] = (
                    to_col(weight0 / total) * part[0, head].astype(jnp.float32)
                    + to_col(weight1 / total) * part[1, head].astype(jnp.float32)
                ).astype(jnp.bfloat16)
                result_copy(head).start()

            loop(0, half, merge)

        loop(0, held, finish)
        loop(0, half * held, lambda head: result_copy(head).wait())


def by_head(qkv, routes):
    tok, heads, width = qkv.shape
    size = width // 3
    nseq = lax.axis_size("seq")
    half = nseq // 2
    held = heads // half
    group = 2 if half % 2 == 0 else 1
    lines = jnp.transpose(routes, (1, 0)).reshape(half, held, tok)
    lines = jnp.pad(lines, ((0, 0), (0, LABEL_ROWS - held), (0, 0)))
    dma = pltpu.SemaphoreType.DMA
    out = pl.pallas_call(
        functools.partial(exchange_kernel, nseq, held, group),
        out_shape=jax.ShapeDtypeStruct((heads, tok, size), jnp.bfloat16),
        in_specs=[pl.BlockSpec(memory_space=pl.ANY)] * 2,
        out_specs=pl.BlockSpec(memory_space=pl.ANY),
        scratch_shapes=[
            pltpu.VMEM((held, half, tok, width), jnp.bfloat16),
            pltpu.VMEM((held, half, tok, size), jnp.bfloat16),
            pltpu.VMEM((nseq, LABEL_ROWS, tok), jnp.int32),
            pltpu.VMEM((held, nseq, tok, size), jnp.bfloat16),
            pltpu.VMEM((held, nseq, 8, tok), jnp.float32),
            pltpu.VMEM((2, heads, tok, size), jnp.bfloat16),
            pltpu.VMEM((2, half, held, 8, tok), jnp.float32),
            pltpu.VMEM((heads, tok, size), jnp.bfloat16),
            pltpu.VMEM((nseq, tok, size), jnp.bfloat16),
            pltpu.VMEM((half, tok, size), jnp.bfloat16),
            dma((held, half)),
            dma((held, half)),
            dma((held, half)),
            dma((held, half)),
            dma((nseq,)),
            dma((nseq,)),
            dma((held, nseq)),
            dma((2, held, half)),
            dma((held, nseq)),
            dma((2, held, half)),
            dma((held,)),
            dma((1,)),
            dma((held,)),
            dma((held,)),
            dma((heads,)),
        ],
        compiler_params=pltpu.CompilerParams(
            collective_id=0, has_side_effects=True, vmem_limit_bytes=48 * 2**20
        ),
        name="exchange",
    )(jnp.transpose(qkv, (1, 0, 2)), lines)
    return jnp.transpose(out, (1, 0, 2))


def solution(mesh):
    placed = (P(("groups", "seq"), None, None), P(("groups", "seq"), None))
    nseq = mesh.shape["seq"]

    def local(qkv, routes):
        heads = qkv.shape[1]
        half = nseq // 2
        clusters = nseq * qkv.shape[0] // CLEN
        fits = clusters <= qkv.shape[2] // 3
        if fits and nseq % 2 == 0 and heads % half == 0 and heads // half <= LABEL_ROWS:
            return by_head(qkv, routes)
        return routed(qkv, routes)

    return jax.shard_map(
        local,
        mesh=mesh,
        in_specs=placed,
        out_specs=P(("groups", "seq"), None, None),
        check_vma=False,
    )
```

```python
import functools
import math

import jax
import jax.numpy as jnp
from jax import lax
from jax.experimental import pallas as pl
from jax.experimental.pallas import tpu as pltpu
from jax.sharding import PartitionSpec as P

CLEN = 1024
LABEL_ROWS = 8
NEG = -1e36


def entering(part, axis, combine, identity):
    place = lax.axis_index(axis)
    gathered = lax.all_gather(part, axis)
    state = jnp.zeros_like(part) + jnp.asarray(identity, part.dtype)

    def one(turn, state):
        return combine(state, lax.dynamic_index_in_dim(gathered, turn, 0, False))

    return lax.fori_loop(0, place, one, state)


def attend(queries, keys, values, start, scale):
    block_rows = queries.shape[1]
    span = keys.shape[1]
    scores = jnp.einsum("pqd,pkd->pqk", queries, keys, preferred_element_type=jnp.float32) * scale
    rows = start + jnp.arange(block_rows, dtype=jnp.int32)[:, None]
    cols = jnp.arange(span, dtype=jnp.int32)[None, :]
    scores = jnp.where((cols <= rows)[None], scores, -1e30)
    peak = jnp.max(scores, axis=2, keepdims=True)
    expo = jnp.exp(scores - peak)
    weights = (expo / jnp.sum(expo, axis=2, keepdims=True)).astype(jnp.bfloat16)
    return jnp.einsum("pqk,pkd->pqd", weights, values, preferred_element_type=jnp.float32).astype(
        jnp.bfloat16
    )


def routed(qkv, routes):
    tok, heads, width = qkv.shape
    head_size = width // 3
    nseq = lax.axis_size("seq")
    clusters = nseq * tok // CLEN
    pairs_dev = heads * tok // CLEN
    capacity = 3 * CLEN // 2
    block_rows = CLEN // 2
    share = CLEN // nseq
    rows_peer = pairs_dev * share
    total_pairs = heads * clusters
    scale = 1.0 / math.sqrt(head_size)
    member = routes[:, :, None] == jnp.arange(clusters, dtype=jnp.int32)[None, None, :]
    member_flat = member.reshape(tok, total_pairs)
    counts = jnp.sum(member_flat.astype(jnp.int32), axis=0)
    earlier = (jnp.arange(tok)[:, None] > jnp.arange(tok)[None, :]).astype(jnp.bfloat16)
    before = jnp.dot(earlier, member_flat.astype(jnp.bfloat16), preferred_element_type=jnp.float32)
    rank = jnp.sum(jnp.where(member, before.reshape(tok, heads, clusters), 0.0), axis=2).astype(
        jnp.int32
    )
    prefix = entering(counts, "seq", lambda first, second: first + second, jnp.zeros_like(counts))

    def lookup(table):
        return jnp.sum(jnp.where(member, table.reshape(heads, clusters)[None], 0), axis=2)

    group_counts = counts.reshape(total_pairs // pairs_dev, pairs_dev)
    within = (jnp.cumsum(group_counts, axis=1) - group_counts).reshape(total_pairs)
    slot = lookup(prefix) + rank
    pair_index = jnp.arange(heads, dtype=jnp.int32)[None, :] * clusters + routes
    owner = pair_index // pairs_dev
    local_pair = pair_index % pairs_dev
    position = (owner * rows_peer + lookup(within) + rank).reshape(tok * heads)
    target = (local_pair * capacity + slot).reshape(tok * heads)
    outgoing = (
        jnp.zeros((tok * heads, width), jnp.bfloat16)
        .at[position]
        .set(qkv.reshape(tok * heads, width))
    )
    labels = jnp.zeros((tok * heads,), jnp.int32).at[position].set(target)
    arrived, places = (
        lax.all_to_all(outgoing, "seq", split_axis=0, concat_axis=0, tiled=True),
        lax.all_to_all(labels, "seq", split_axis=0, concat_axis=0, tiled=True),
    )
    tiles = jnp.zeros((pairs_dev * capacity, width), jnp.bfloat16).at[places].set(arrived)
    tiles = tiles.reshape(pairs_dev, capacity, width)
    pieces = []
    for index in range(3):
        start = index * block_rows
        stop = start + block_rows
        pieces.append(
            attend(
                tiles[:, start:stop, :head_size],
                tiles[:, :stop, head_size : 2 * head_size],
                tiles[:, :stop, 2 * head_size :],
                start,
                scale,
            )
        )
    results = jnp.concatenate(pieces, axis=1)
    flat_results = results.reshape(pairs_dev * capacity, head_size)
    replies = flat_results[places]
    returned = lax.all_to_all(replies, "seq", split_axis=0, concat_axis=0, tiled=True)
    return returned[position].reshape(tok, heads, head_size)


def partial_softmax(query, keys, values, scale, causal):
    rows = query.shape[0]
    span = keys.shape[0]
    size = values.shape[1] // 2
    contract = (((1,), (1,)), ((), ()))
    scores = lax.dot_general(query, keys, contract, preferred_element_type=jnp.float32)
    if causal:
        past = span - rows
        row_id = lax.broadcasted_iota(jnp.int32, (rows, rows), 0)
        col_id = lax.broadcasted_iota(jnp.int32, (rows, rows), 1)
        last = jnp.where(col_id <= row_id, scores[:, past:], NEG)
        scores = jnp.concatenate([scores[:, :past], last], axis=1) if past else last
    factor = scale * math.log2(math.e)
    peak = jnp.max(scores, axis=1, keepdims=True) * factor
    expo = jnp.exp2(scores * factor - peak).astype(jnp.bfloat16)
    out = jnp.dot(expo, values, preferred_element_type=jnp.float32)
    total = out[:, size:]
    return (out[:, :size] / total).astype(jnp.bfloat16), peak, total[:, :1]


def exchange_kernel(
    nseq, held, group, x_ref, lab_ref, out_ref, recv, qrecv, labs, obuf, sbuf, part, stats, merged, hot, cold,
    x_send, x_recv, q_send, q_recv, l_send, l_recv, o_send, o_recv, s_send, s_recv,
    own_x, own_l, own_o, own_s, m_sem,
):
    me = lax.axis_index("seq")
    half = nseq // 2
    low = me < half
    up = me >= half
    side = me // half
    base = side * half
    mine = lax.rem(me, half)
    tok, width = x_ref.shape[1:]
    size = width // 3
    scale = 1.0 / math.sqrt(size)
    rows = group * tok
    ahead = 1
    wide = 2 * group if half % (2 * group) == 0 else group

    def remote(src, dst, send, recv_sem, peer):
        return pltpu.make_async_remote_copy(
            src_ref=src, dst_ref=dst, send_sem=send, recv_sem=recv_sem,
            device_id={"seq": peer}, device_id_type=pl.DeviceIdType.MESH,
        )

    def x_copy(j, p):
        return remote(x_ref.at[p * held + j], recv.at[j, mine],
                      x_send.at[j, p], x_recv.at[j, mine], base + p)

    def x_arrival(j, p):
        return remote(x_ref.at[0], recv.at[j, p], x_send.at[j, p], x_recv.at[j, p], base + p)

    def q_copy(j, p):
        return remote(x_ref.at[p * held + j, :, pl.ds(0, size)], qrecv.at[j, mine],
                      q_send.at[j, p], q_recv.at[j, mine], p)

    def q_arrival(j, p):
        return remote(x_ref.at[0, :, pl.ds(0, size)], qrecv.at[j, p],
                      q_send.at[j, p], q_recv.at[j, p], half + p)

    def l_copy(peer):
        return remote(lab_ref.at[lax.rem(peer, half)], labs.at[me],
                      l_send.at[peer], l_recv.at[me], peer)

    def l_arrival(peer):
        return remote(lab_ref.at[0], labs.at[peer], l_send.at[peer], l_recv.at[peer], peer)

    def o_copy_low(j, p):
        return remote(obuf.at[j, p], out_ref.at[mine * held + j],
                      o_send.at[j, p], o_recv.at[0, j, mine], p)

    def o_arrival_low(j, p):
        return remote(obuf.at[j, 0], out_ref.at[p * held + j],
                      o_send.at[j, p], o_recv.at[0, j, p], p)

    def o_copy_up(j, peer):
        return remote(obuf.at[j, peer], part.at[side, mine * held + j],
                      o_send.at[j, peer], o_recv.at[side, j, mine], peer)

    def o_arrival_up(which, j, p):
        return remote(obuf.at[j, 0], part.at[which, p * held + j],
                      o_send.at[j, which * half + p], o_recv.at[which, j, p], which * half + p)

    def s_copy(j, peer):
        return remote(sbuf.at[j, peer], stats.at[side, mine, j],
                      s_send.at[j, peer], s_recv.at[side, j, mine], peer)

    def s_arrival(which, j, p):
        return remote(sbuf.at[j, 0], stats.at[which, p, j],
                      s_send.at[j, which * half + p], s_recv.at[which, j, p], which * half + p)

    def own_x_copy(j):
        return pltpu.make_async_copy(x_ref.at[mine * held + j], recv.at[j, mine], own_x.at[j])

    def own_o_low(j):
        return pltpu.make_async_copy(obuf.at[j, me], out_ref.at[mine * held + j], own_o.at[j])

    def own_o_up(j):
        return pltpu.make_async_copy(obuf.at[j, me], part.at[1, mine * held + j], own_o.at[j])

    def own_s_up(j):
        return pltpu.make_async_copy(sbuf.at[j, me], stats.at[1, mine, j], own_s.at[j])

    def result_copy(head):
        return pltpu.make_async_copy(merged.at[head], out_ref.at[head], m_sem.at[head])

    own_lab = pltpu.make_async_copy(lab_ref.at[mine], labs.at[me], own_l.at[0])

    def loop(start, stop, body):
        def step(k, carry):
            body(k)
            return carry

        lax.fori_loop(start, stop, step, 0)

    def each_peer(body):
        loop(1, nseq, lambda k: body(lax.rem(me + k, nseq)))

    def each_near(body):
        loop(1, half, lambda k: body(lax.rem(mine + k, half)))

    def each_far(body):
        loop(0, half, lambda k: body(lax.rem(mine + k, half)))

    own_lab.start()
    for j in range(held):
        own_x_copy(j).start()
    barrier = pltpu.get_barrier_semaphore()
    each_peer(lambda peer: pl.semaphore_signal(
        barrier, inc=1, device_id={"seq": peer}, device_id_type=pl.DeviceIdType.MESH))
    pl.semaphore_wait(barrier, nseq - 1)

    each_near(lambda p: l_copy(base + p).start())

    @pl.when(up)
    def _():
        each_far(lambda p: l_copy(p).start())

    def send_chunk(j):
        @pl.when(up)
        def _():
            each_far(lambda p: q_copy(j, p).start())

        each_near(lambda p: x_copy(j, p).start())

    loop(0, min(ahead, held), send_chunk)
    own_lab.wait()
    for j in range(held):
        own_x_copy(j).wait()
    each_near(lambda p: l_arrival(base + p).wait_recv())

    @pl.when(low)
    def _():
        each_far(lambda p: l_arrival(half + p).wait_recv())

    eye = lax.broadcasted_iota(jnp.int32, (tok, tok), 0) == lax.broadcasted_iota(
        jnp.int32, (tok, tok), 1)

    def to_col(line):
        return jnp.sum(jnp.where(eye, line, jnp.zeros_like(line)), axis=1, keepdims=True)

    def to_row(col):
        return jnp.sum(jnp.where(eye, col, jnp.zeros_like(col)), axis=0, keepdims=True)

    def keep(j, first, count, result, peak, total):
        for g in range(count):
            part_rows = slice(g * tok, (g + 1) * tok)
            obuf[j, first + g] = result[part_rows]
            sbuf[j, first + g, 0:1, :] = to_row(peak[part_rows])
            sbuf[j, first + g, 1:2, :] = to_row(total[part_rows])

    def chunk(j):
        def label_match(source):
            col = to_col(labs[source, pl.ds(j, 1), :])
            return lax.broadcasted_iota(jnp.int32, (tok, size), 1) == col

        def fill_near(p):
            match = label_match(base + p)
            hot[base + p] = jnp.where(match, 1.0, 0.0).astype(jnp.bfloat16)
            cold[p] = jnp.where(match, 0.0, NEG).astype(jnp.bfloat16)

        loop(0, half, fill_near)
        each_near(lambda p: x_arrival(j, p).wait_recv())

        @pl.when(low)
        def _():
            each_far(lambda p: q_arrival(j, p).wait_recv())

        @pl.when(j + ahead < held)
        def _():
            send_chunk(j + ahead)

        def keys_of(span):
            keys = recv[j, :span, :, size : 2 * size].reshape(span * tok, size)
            return jnp.concatenate([keys, cold[:span].reshape(span * tok, size)], axis=1)

        def values_of(span):
            values = recv[j, :span, :, 2 * size :].reshape(span * tok, size)
            return jnp.concatenate([values, jnp.ones((span * tok, size), jnp.bfloat16)], axis=1)

        @pl.when(low)
        def _():
            def fill_far(p):
                hot[half + p] = jnp.where(label_match(half + p), 1.0, 0.0).astype(jnp.bfloat16)

            loop(0, half, fill_far)
            for first in range(0, half, wide):
                query = jnp.concatenate([
                    qrecv[j, first : first + wide].reshape(wide * tok, size),
                    hot[half + first : half + first + wide].reshape(wide * tok, size)], axis=1)
                result, peak, total = partial_softmax(
                    query, keys_of(half), values_of(half), scale, False)
                keep(j, half + first, wide, result, peak, total)
                for g in range(wide):
                    o_copy_up(j, half + first + g).start()
                    s_copy(j, half + first + g).start()

        for first in range(0, half, group):
            query = jnp.concatenate([
                recv[j, first : first + group, :, :size].reshape(rows, size),
                hot[pl.ds(base + first, group)].reshape(rows, size)], axis=1)
            result, peak, total = partial_softmax(
                query, keys_of(first + group), values_of(first + group), scale, True)
            keep(j, base + first, group, result, peak, total)

        @pl.when(low)
        def _():
            each_near(lambda p: o_copy_low(j, p).start())
            own_o_low(j).start()

        @pl.when(up)
        def _():
            def send_up(p):
                o_copy_up(j, half + p).start()
                s_copy(j, half + p).start()

            each_near(send_up)
            own_o_up(j).start()
            own_s_up(j).start()

    loop(0, held, chunk)

    each_near(lambda p: l_copy(base + p).wait_send())
    loop(0, held, lambda j: each_near(lambda p: x_copy(j, p).wait_send()))

    @pl.when(low)
    def _():
        def finish(j):
            own_o_low(j).wait()

            def near(p):
                o_copy_low(j, p).wait_send()
                o_arrival_low(j, p).wait_recv()

            def far(p):
                o_copy_up(j, half + p).wait_send()
                s_copy(j, half + p).wait_send()

            each_near(near)
            each_far(far)

        loop(0, held, finish)

    @pl.when(up)
    def _():
        each_far(lambda p: l_copy(p).wait_send())
        loop(0, held, lambda j: each_far(lambda p: q_copy(j, p).wait_send()))

        def finish(j):
            own_o_up(j).wait()
            own_s_up(j).wait()

            def near(p):
                o_copy_up(j, half + p).wait_send()
                s_copy(j, half + p).wait_send()
                o_arrival_up(1, j, p).wait_recv()
                s_arrival(1, j, p).wait_recv()

            each_near(near)

            def merge(p):
                o_arrival_up(0, j, p).wait_recv()
                s_arrival(0, j, p).wait_recv()
                head = p * held + j
                peak0, peak1 = stats[0, p, j, 0:1, :], stats[1, p, j, 0:1, :]
                peak = jnp.maximum(peak0, peak1)
                weight0 = stats[0, p, j, 1:2, :] * jnp.exp2(peak0 - peak)
                weight1 = stats[1, p, j, 1:2, :] * jnp.exp2(peak1 - peak)
                total = weight0 + weight1
                merged[head] = (
                    to_col(weight0 / total) * part[0, head].astype(jnp.float32)
                    + to_col(weight1 / total) * part[1, head].astype(jnp.float32)
                ).astype(jnp.bfloat16)
                result_copy(head).start()

            loop(0, half, merge)

        loop(0, held, finish)
        loop(0, half * held, lambda head: result_copy(head).wait())


def by_head(qkv, routes):
    tok, heads, width = qkv.shape
    size = width // 3
    nseq = lax.axis_size("seq")
    half = nseq // 2
    held = heads // half
    group = 2 if half % 2 == 0 else 1
    lines = jnp.transpose(routes, (1, 0)).reshape(half, held, tok)
    lines = jnp.pad(lines, ((0, 0), (0, LABEL_ROWS - held), (0, 0)))
    dma = pltpu.SemaphoreType.DMA
    out = pl.pallas_call(
        functools.partial(exchange_kernel, nseq, held, group),
        out_shape=jax.ShapeDtypeStruct((heads, tok, size), jnp.bfloat16),
        in_specs=[pl.BlockSpec(memory_space=pl.ANY)] * 2,
        out_specs=pl.BlockSpec(memory_space=pl.ANY),
        scratch_shapes=[
            pltpu.VMEM((held, half, tok, width), jnp.bfloat16),
            pltpu.VMEM((held, half, tok, size), jnp.bfloat16),
            pltpu.VMEM((nseq, LABEL_ROWS, tok), jnp.int32),
            pltpu.VMEM((held, nseq, tok, size), jnp.bfloat16),
            pltpu.VMEM((held, nseq, 8, tok), jnp.float32),
            pltpu.VMEM((2, heads, tok, size), jnp.bfloat16),
            pltpu.VMEM((2, half, held, 8, tok), jnp.float32),
            pltpu.VMEM((heads, tok, size), jnp.bfloat16),
            pltpu.VMEM((nseq, tok, size), jnp.bfloat16),
            pltpu.VMEM((half, tok, size), jnp.bfloat16),
            dma((held, half)),
            dma((held, half)),
            dma((held, half)),
            dma((held, half)),
            dma((nseq,)),
            dma((nseq,)),
            dma((held, nseq)),
            dma((2, held, half)),
            dma((held, nseq)),
            dma((2, held, half)),
            dma((held,)),
            dma((1,)),
            dma((held,)),
            dma((held,)),
            dma((heads,)),
        ],
        compiler_params=pltpu.CompilerParams(
            collective_id=0, has_side_effects=True, vmem_limit_bytes=48 * 2**20
        ),
        name="exchange",
    )(jnp.transpose(qkv, (1, 0, 2)), lines)
    return jnp.transpose(out, (1, 0, 2))


def solution(mesh):
    placed = (P(("groups", "seq"), None, None), P(("groups", "seq"), None))
    nseq = mesh.shape["seq"]

    def local(qkv, routes):
        heads = qkv.shape[1]
        half = nseq // 2
        clusters = nseq * qkv.shape[0] // CLEN
        fits = clusters <= qkv.shape[2] // 3
        if fits and nseq % 2 == 0 and heads % half == 0 and heads // half <= LABEL_ROWS:
            return by_head(qkv, routes)
        return routed(qkv, routes)

    return jax.shard_map(
        local,
        mesh=mesh,
        in_specs=placed,
        out_specs=P(("groups", "seq"), None, None),
        check_vma=False,
    )
```

```python
import functools
import math

import jax
import jax.numpy as jnp
from jax import lax
from jax.experimental import pallas as pl
from jax.experimental.pallas import tpu as pltpu
from jax.sharding import PartitionSpec as P

CLEN = 1024
NEG = -1e36


def entering(part, axis, combine, identity):
    place = lax.axis_index(axis)
    gathered = lax.all_gather(part, axis)
    state = jnp.zeros_like(part) + jnp.asarray(identity, part.dtype)

    def one(turn, state):
        return combine(state, lax.dynamic_index_in_dim(gathered, turn, 0, False))

    return lax.fori_loop(0, place, one, state)


def attend(queries, keys, values, start, scale):
    block_rows = queries.shape[1]
    span = keys.shape[1]
    scores = jnp.einsum("pqd,pkd->pqk", queries, keys, preferred_element_type=jnp.float32) * scale
    rows = start + jnp.arange(block_rows, dtype=jnp.int32)[:, None]
    cols = jnp.arange(span, dtype=jnp.int32)[None, :]
    scores = jnp.where((cols <= rows)[None], scores, -1e30)
    peak = jnp.max(scores, axis=2, keepdims=True)
    expo = jnp.exp(scores - peak)
    weights = (expo / jnp.sum(expo, axis=2, keepdims=True)).astype(jnp.bfloat16)
    return jnp.einsum("pqk,pkd->pqd", weights, values, preferred_element_type=jnp.float32).astype(
        jnp.bfloat16
    )


def routed(qkv, routes):
    tok, heads, width = qkv.shape
    head_size = width // 3
    nseq = lax.axis_size("seq")
    clusters = nseq * tok // CLEN
    pairs_dev = heads * tok // CLEN
    capacity = 3 * CLEN // 2
    block_rows = CLEN // 2
    share = CLEN // nseq
    rows_peer = pairs_dev * share
    total_pairs = heads * clusters
    scale = 1.0 / math.sqrt(head_size)
    member = routes[:, :, None] == jnp.arange(clusters, dtype=jnp.int32)[None, None, :]
    member_flat = member.reshape(tok, total_pairs)
    counts = jnp.sum(member_flat.astype(jnp.int32), axis=0)
    earlier = (jnp.arange(tok)[:, None] > jnp.arange(tok)[None, :]).astype(jnp.bfloat16)
    before = jnp.dot(earlier, member_flat.astype(jnp.bfloat16), preferred_element_type=jnp.float32)
    rank = jnp.sum(jnp.where(member, before.reshape(tok, heads, clusters), 0.0), axis=2).astype(
        jnp.int32
    )
    prefix = entering(counts, "seq", lambda first, second: first + second, jnp.zeros_like(counts))

    def lookup(table):
        return jnp.sum(jnp.where(member, table.reshape(heads, clusters)[None], 0), axis=2)

    group_counts = counts.reshape(total_pairs // pairs_dev, pairs_dev)
    within = (jnp.cumsum(group_counts, axis=1) - group_counts).reshape(total_pairs)
    slot = lookup(prefix) + rank
    pair_index = jnp.arange(heads, dtype=jnp.int32)[None, :] * clusters + routes
    owner = pair_index // pairs_dev
    local_pair = pair_index % pairs_dev
    position = (owner * rows_peer + lookup(within) + rank).reshape(tok * heads)
    target = (local_pair * capacity + slot).reshape(tok * heads)
    outgoing = (
        jnp.zeros((tok * heads, width), jnp.bfloat16)
        .at[position]
        .set(qkv.reshape(tok * heads, width))
    )
    labels = jnp.zeros((tok * heads,), jnp.int32).at[position].set(target)
    arrived, places = (
        lax.all_to_all(outgoing, "seq", split_axis=0, concat_axis=0, tiled=True),
        lax.all_to_all(labels, "seq", split_axis=0, concat_axis=0, tiled=True),
    )
    tiles = jnp.zeros((pairs_dev * capacity, width), jnp.bfloat16).at[places].set(arrived)
    tiles = tiles.reshape(pairs_dev, capacity, width)
    pieces = []
    for index in range(3):
        start = index * block_rows
        stop = start + block_rows
        pieces.append(
            attend(
                tiles[:, start:stop, :head_size],
                tiles[:, :stop, head_size : 2 * head_size],
                tiles[:, :stop, 2 * head_size :],
                start,
                scale,
            )
        )
    results = jnp.concatenate(pieces, axis=1)
    flat_results = results.reshape(pairs_dev * capacity, head_size)
    replies = flat_results[places]
    returned = lax.all_to_all(replies, "seq", split_axis=0, concat_axis=0, tiled=True)
    return returned[position].reshape(tok, heads, head_size)


def partial_softmax(query, keys, values, scale, causal):
    rows = query.shape[0]
    span = keys.shape[0]
    size = values.shape[1] // 2
    contract = (((1,), (1,)), ((), ()))
    scores = lax.dot_general(query, keys, contract, preferred_element_type=jnp.float32)
    if causal:
        past = span - rows
        row_id = lax.broadcasted_iota(jnp.int32, (rows, rows), 0)
        col_id = lax.broadcasted_iota(jnp.int32, (rows, rows), 1)
        last = jnp.where(col_id <= row_id, scores[:, past:], NEG)
        scores = jnp.concatenate([scores[:, :past], last], axis=1) if past else last
    factor = scale * math.log2(math.e)
    peak = jnp.max(scores, axis=1, keepdims=True) * factor
    expo = jnp.exp2(scores * factor - peak).astype(jnp.bfloat16)
    out = jnp.dot(expo, values, preferred_element_type=jnp.float32)
    total = out[:, size:]
    return (out[:, :size] / total).astype(jnp.bfloat16), peak, total[:, :1]


def exchange_kernel(
    nseq, held, group, x_ref, lab_ref, out_ref, recv, qrecv, labs, obuf, sbuf, part, stats, merged, hot, cold,
    x_send, x_recv, q_send, q_recv, l_send, l_recv, o_send, o_recv, s_send, s_recv,
    own_x, own_l, own_o, own_s, m_sem,
):
    me = lax.axis_index("seq")
    half = nseq // 2
    low = me < half
    up = me >= half
    side = me // half
    base = side * half
    mine = lax.rem(me, half)
    tok, width = x_ref.shape[1:]
    size = width // 3
    scale = 1.0 / math.sqrt(size)
    rows = group * tok
    ahead = 2
    wide = 2 * group if half % (2 * group) == 0 else group

    def remote(src, dst, send, recv_sem, peer):
        return pltpu.make_async_remote_copy(
            src_ref=src, dst_ref=dst, send_sem=send, recv_sem=recv_sem,
            device_id={"seq": peer}, device_id_type=pl.DeviceIdType.MESH,
        )

    def x_copy(j, p):
        return remote(x_ref.at[p * held + j], recv.at[j, mine],
                      x_send.at[j, p], x_recv.at[j, mine], base + p)

    def x_arrival(j, p):
        return remote(x_ref.at[0], recv.at[j, p], x_send.at[j, p], x_recv.at[j, p], base + p)

    def q_copy(j, p):
        return remote(x_ref.at[p * held + j, :, pl.ds(0, size)], qrecv.at[j, mine],
                      q_send.at[j, p], q_recv.at[j, mine], p)

    def q_arrival(j, p):
        return remote(x_ref.at[0, :, pl.ds(0, size)], qrecv.at[j, p],
                      q_send.at[j, p], q_recv.at[j, p], half + p)

    def l_copy(peer):
        return remote(lab_ref.at[lax.rem(peer, half)], labs.at[me],
                      l_send.at[peer], l_recv.at[me], peer)

    def l_arrival(peer):
        return remote(lab_ref.at[0], labs.at[peer], l_send.at[peer], l_recv.at[peer], peer)

    def o_copy_low(j, p):
        return remote(obuf.at[j, p], out_ref.at[mine * held + j],
                      o_send.at[j, p], o_recv.at[0, j, mine], p)

    def o_arrival_low(j, p):
        return remote(obuf.at[j, 0], out_ref.at[p * held + j],
                      o_send.at[j, p], o_recv.at[0, j, p], p)

    def o_copy_up(j, peer):
        return remote(obuf.at[j, peer], part.at[side, mine * held + j],
                      o_send.at[j, peer], o_recv.at[side, j, mine], peer)

    def o_arrival_up(which, j, p):
        return remote(obuf.at[j, 0], part.at[which, p * held + j],
                      o_send.at[j, which * half + p], o_recv.at[which, j, p], which * half + p)

    def s_copy(j, peer):
        return remote(sbuf.at[j, peer], stats.at[side, mine, j],
                      s_send.at[j, peer], s_recv.at[side, j, mine], peer)

    def s_arrival(which, j, p):
        return remote(sbuf.at[j, 0], stats.at[which, p, j],
                      s_send.at[j, which * half + p], s_recv.at[which, j, p], which * half + p)

    def own_x_copy(j):
        return pltpu.make_async_copy(x_ref.at[mine * held + j], recv.at[j, mine], own_x.at[j])

    def own_o_low(j):
        return pltpu.make_async_copy(obuf.at[j, me], out_ref.at[mine * held + j], own_o.at[j])

    def own_o_up(j):
        return pltpu.make_async_copy(obuf.at[j, me], part.at[1, mine * held + j], own_o.at[j])

    def own_s_up(j):
        return pltpu.make_async_copy(sbuf.at[j, me], stats.at[1, mine, j], own_s.at[j])

    def result_copy(head):
        return pltpu.make_async_copy(merged.at[head], out_ref.at[head], m_sem.at[head])

    own_lab = pltpu.make_async_copy(lab_ref.at[mine], labs.at[me], own_l.at[0])

    def loop(start, stop, body):
        def step(k, carry):
            body(k)
            return carry

        lax.fori_loop(start, stop, step, 0)

    def each_peer(body):
        loop(1, nseq, lambda k: body(lax.rem(me + k, nseq)))

    def each_near(body):
        loop(1, half, lambda k: body(lax.rem(mine + k, half)))

    def each_far(body):
        loop(0, half, lambda k: body(lax.rem(mine + k, half)))

    own_lab.start()
    for j in range(held):
        own_x_copy(j).start()
    barrier = pltpu.get_barrier_semaphore()
    each_peer(lambda peer: pl.semaphore_signal(
        barrier, inc=1, device_id={"seq": peer}, device_id_type=pl.DeviceIdType.MESH))
    pl.semaphore_wait(barrier, nseq - 1)

    each_near(lambda p: l_copy(base + p).start())

    @pl.when(up)
    def _():
        each_far(lambda p: l_copy(p).start())

    def send_chunk(j):
        @pl.when(up)
        def _():
            each_far(lambda p: q_copy(j, p).start())

        each_near(lambda p: x_copy(j, p).start())

    send_chunk(0)
    own_lab.wait()
    for j in range(held):
        own_x_copy(j).wait()
    each_near(lambda p: l_arrival(base + p).wait_recv())

    @pl.when(low)
    def _():
        each_far(lambda p: l_arrival(half + p).wait_recv())

    eye = lax.broadcasted_iota(jnp.int32, (tok, tok), 0) == lax.broadcasted_iota(
        jnp.int32, (tok, tok), 1)

    def to_col(line):
        return jnp.sum(jnp.where(eye, line, jnp.zeros_like(line)), axis=1, keepdims=True)

    def to_row(col):
        return jnp.sum(jnp.where(eye, col, jnp.zeros_like(col)), axis=0, keepdims=True)

    def keep(j, first, count, result, peak, total):
        for g in range(count):
            part_rows = slice(g * tok, (g + 1) * tok)
            obuf[j, first + g] = result[part_rows]
            sbuf[j, first + g, 0:1, :] = to_row(peak[part_rows])
            sbuf[j, first + g, 1:2, :] = to_row(total[part_rows])

    def chunk(j):
        def label_match(source):
            col = to_col(labs[source, pl.ds(j, 1), :])
            return lax.broadcasted_iota(jnp.int32, (tok, size), 1) == col

        def fill_near(p):
            match = label_match(base + p)
            hot[base + p] = jnp.where(match, 1.0, 0.0).astype(jnp.bfloat16)
            cold[p] = jnp.where(match, 0.0, NEG).astype(jnp.bfloat16)

        loop(0, half, fill_near)
        each_near(lambda p: x_arrival(j, p).wait_recv())

        @pl.when(low)
        def _():
            each_far(lambda p: q_arrival(j, p).wait_recv())

        @pl.when(j == 0)
        def _():
            loop(1, min(ahead, held), send_chunk)

        @pl.when(j + ahead < held)
        def _():
            send_chunk(j + ahead)

        def keys_of(span):
            keys = recv[j, :span, :, size : 2 * size].reshape(span * tok, size)
            return jnp.concatenate([keys, cold[:span].reshape(span * tok, size)], axis=1)

        def values_of(span):
            values = recv[j, :span, :, 2 * size :].reshape(span * tok, size)
            return jnp.concatenate([values, jnp.ones((span * tok, size), jnp.bfloat16)], axis=1)

        @pl.when(low)
        def _():
            def fill_far(p):
                hot[half + p] = jnp.where(label_match(half + p), 1.0, 0.0).astype(jnp.bfloat16)

            loop(0, half, fill_far)
            for first in range(0, half, wide):
                query = jnp.concatenate([
                    qrecv[j, first : first + wide].reshape(wide * tok, size),
                    hot[half + first : half + first + wide].reshape(wide * tok, size)], axis=1)
                result, peak, total = partial_softmax(
                    query, keys_of(half), values_of(half), scale, False)
                keep(j, half + first, wide, result, peak, total)
                for g in range(wide):
                    o_copy_up(j, half + first + g).start()
                    s_copy(j, half + first + g).start()

        for first in range(0, half, group):
            query = jnp.concatenate([
                recv[j, first : first + group, :, :size].reshape(rows, size),
                hot[pl.ds(base + first, group)].reshape(rows, size)], axis=1)
            result, peak, total = partial_softmax(
                query, keys_of(first + group), values_of(first + group), scale, True)
            keep(j, base + first, group, result, peak, total)

        @pl.when(low)
        def _():
            each_near(lambda p: o_copy_low(j, p).start())
            own_o_low(j).start()

        @pl.when(up)
        def _():
            def send_up(p):
                o_copy_up(j, half + p).start()
                s_copy(j, half + p).start()

            each_near(send_up)
            own_o_up(j).start()
            own_s_up(j).start()

    loop(0, held, chunk)

    each_near(lambda p: l_copy(base + p).wait_send())
    loop(0, held, lambda j: each_near(lambda p: x_copy(j, p).wait_send()))

    @pl.when(low)
    def _():
        def finish(j):
            own_o_low(j).wait()

            def near(p):
                o_copy_low(j, p).wait_send()
                o_arrival_low(j, p).wait_recv()

            def far(p):
                o_copy_up(j, half + p).wait_send()
                s_copy(j, half + p).wait_send()

            each_near(near)
            each_far(far)

        loop(0, held, finish)

    @pl.when(up)
    def _():
        each_far(lambda p: l_copy(p).wait_send())
        loop(0, held, lambda j: each_far(lambda p: q_copy(j, p).wait_send()))

        def finish(j):
            own_o_up(j).wait()
            own_s_up(j).wait()

            def near(p):
                o_copy_up(j, half + p).wait_send()
                s_copy(j, half + p).wait_send()
                o_arrival_up(1, j, p).wait_recv()
                s_arrival(1, j, p).wait_recv()

            each_near(near)

            def merge(p):
                o_arrival_up(0, j, p).wait_recv()
                s_arrival(0, j, p).wait_recv()
                head = p * held + j
                peak0, peak1 = stats[0, p, j, 0:1, :], stats[1, p, j, 0:1, :]
                peak = jnp.maximum(peak0, peak1)
                weight0 = stats[0, p, j, 1:2, :] * jnp.exp2(peak0 - peak)
                weight1 = stats[1, p, j, 1:2, :] * jnp.exp2(peak1 - peak)
                total = weight0 + weight1
                merged[head] = (
                    to_col(weight0 / total) * part[0, head].astype(jnp.float32)
                    + to_col(weight1 / total) * part[1, head].astype(jnp.float32)
                ).astype(jnp.bfloat16)
                result_copy(head).start()

            loop(0, half, merge)

        loop(0, held, finish)
        loop(0, half * held, lambda head: result_copy(head).wait())


def by_head(qkv, routes):
    tok, heads, width = qkv.shape
    size = width // 3
    nseq = lax.axis_size("seq")
    half = nseq // 2
    held = heads // half
    group = 2 if half % 2 == 0 else 1
    lines = jnp.transpose(routes, (1, 0)).reshape(half, held, tok)
    dma = pltpu.SemaphoreType.DMA
    out = pl.pallas_call(
        functools.partial(exchange_kernel, nseq, held, group),
        out_shape=jax.ShapeDtypeStruct((heads, tok, size), jnp.bfloat16),
        in_specs=[pl.BlockSpec(memory_space=pl.ANY)] * 2,
        out_specs=pl.BlockSpec(memory_space=pl.ANY),
        scratch_shapes=[
            pltpu.VMEM((held, half, tok, width), jnp.bfloat16),
            pltpu.VMEM((held, half, tok, size), jnp.bfloat16),
            pltpu.VMEM((nseq, held, tok), jnp.int32),
            pltpu.VMEM((held, nseq, tok, size), jnp.bfloat16),
            pltpu.VMEM((held, nseq, 8, tok), jnp.float32),
            pltpu.VMEM((2, heads, tok, size), jnp.bfloat16),
            pltpu.VMEM((2, half, held, 8, tok), jnp.float32),
            pltpu.VMEM((heads, tok, size), jnp.bfloat16),
            pltpu.VMEM((nseq, tok, size), jnp.bfloat16),
            pltpu.VMEM((half, tok, size), jnp.bfloat16),
            dma((held, half)),
            dma((held, half)),
            dma((held, half)),
            dma((held, half)),
            dma((nseq,)),
            dma((nseq,)),
            dma((held, nseq)),
            dma((2, held, half)),
            dma((held, nseq)),
            dma((2, held, half)),
            dma((held,)),
            dma((1,)),
            dma((held,)),
            dma((held,)),
            dma((heads,)),
        ],
        compiler_params=pltpu.CompilerParams(
            collective_id=0, has_side_effects=True, vmem_limit_bytes=48 * 2**20
        ),
        name="exchange",
    )(jnp.transpose(qkv, (1, 0, 2)), lines)
    return jnp.transpose(out, (1, 0, 2))


def solution(mesh):
    placed = (P(("groups", "seq"), None, None), P(("groups", "seq"), None))
    nseq = mesh.shape["seq"]

    def local(qkv, routes):
        heads = qkv.shape[1]
        half = nseq // 2
        clusters = nseq * qkv.shape[0] // CLEN
        fits = clusters <= qkv.shape[2] // 3
        if fits and nseq % 2 == 0 and heads % half == 0:
            return by_head(qkv, routes)
        return routed(qkv, routes)

    return jax.shard_map(
        local,
        mesh=mesh,
        in_specs=placed,
        out_specs=P(("groups", "seq"), None, None),
        check_vma=False,
    )
```

```python
import functools
import math

import jax
import jax.numpy as jnp
from jax import lax
from jax.experimental import pallas as pl
from jax.experimental.pallas import tpu as pltpu
from jax.sharding import PartitionSpec as P

CLEN = 1024
NEG = -1e36


def entering(part, axis, combine, identity):
    place = lax.axis_index(axis)
    gathered = lax.all_gather(part, axis)
    state = jnp.zeros_like(part) + jnp.asarray(identity, part.dtype)

    def one(turn, state):
        return combine(state, lax.dynamic_index_in_dim(gathered, turn, 0, False))

    return lax.fori_loop(0, place, one, state)


def attend(queries, keys, values, start, scale):
    block_rows = queries.shape[1]
    span = keys.shape[1]
    scores = jnp.einsum("pqd,pkd->pqk", queries, keys, preferred_element_type=jnp.float32) * scale
    rows = start + jnp.arange(block_rows, dtype=jnp.int32)[:, None]
    cols = jnp.arange(span, dtype=jnp.int32)[None, :]
    scores = jnp.where((cols <= rows)[None], scores, -1e30)
    peak = jnp.max(scores, axis=2, keepdims=True)
    expo = jnp.exp(scores - peak)
    weights = (expo / jnp.sum(expo, axis=2, keepdims=True)).astype(jnp.bfloat16)
    return jnp.einsum("pqk,pkd->pqd", weights, values, preferred_element_type=jnp.float32).astype(
        jnp.bfloat16
    )


def routed(qkv, routes):
    tok, heads, width = qkv.shape
    head_size = width // 3
    nseq = lax.axis_size("seq")
    clusters = nseq * tok // CLEN
    pairs_dev = heads * tok // CLEN
    capacity = 3 * CLEN // 2
    block_rows = CLEN // 2
    share = CLEN // nseq
    rows_peer = pairs_dev * share
    total_pairs = heads * clusters
    scale = 1.0 / math.sqrt(head_size)
    member = routes[:, :, None] == jnp.arange(clusters, dtype=jnp.int32)[None, None, :]
    member_flat = member.reshape(tok, total_pairs)
    counts = jnp.sum(member_flat.astype(jnp.int32), axis=0)
    earlier = (jnp.arange(tok)[:, None] > jnp.arange(tok)[None, :]).astype(jnp.bfloat16)
    before = jnp.dot(earlier, member_flat.astype(jnp.bfloat16), preferred_element_type=jnp.float32)
    rank = jnp.sum(jnp.where(member, before.reshape(tok, heads, clusters), 0.0), axis=2).astype(
        jnp.int32
    )
    prefix = entering(counts, "seq", lambda first, second: first + second, jnp.zeros_like(counts))

    def lookup(table):
        return jnp.sum(jnp.where(member, table.reshape(heads, clusters)[None], 0), axis=2)

    group_counts = counts.reshape(total_pairs // pairs_dev, pairs_dev)
    within = (jnp.cumsum(group_counts, axis=1) - group_counts).reshape(total_pairs)
    slot = lookup(prefix) + rank
    pair_index = jnp.arange(heads, dtype=jnp.int32)[None, :] * clusters + routes
    owner = pair_index // pairs_dev
    local_pair = pair_index % pairs_dev
    position = (owner * rows_peer + lookup(within) + rank).reshape(tok * heads)
    target = (local_pair * capacity + slot).reshape(tok * heads)
    outgoing = (
        jnp.zeros((tok * heads, width), jnp.bfloat16)
        .at[position]
        .set(qkv.reshape(tok * heads, width))
    )
    labels = jnp.zeros((tok * heads,), jnp.int32).at[position].set(target)
    arrived, places = (
        lax.all_to_all(outgoing, "seq", split_axis=0, concat_axis=0, tiled=True),
        lax.all_to_all(labels, "seq", split_axis=0, concat_axis=0, tiled=True),
    )
    tiles = jnp.zeros((pairs_dev * capacity, width), jnp.bfloat16).at[places].set(arrived)
    tiles = tiles.reshape(pairs_dev, capacity, width)
    pieces = []
    for index in range(3):
        start = index * block_rows
        stop = start + block_rows
        pieces.append(
            attend(
                tiles[:, start:stop, :head_size],
                tiles[:, :stop, head_size : 2 * head_size],
                tiles[:, :stop, 2 * head_size :],
                start,
                scale,
            )
        )
    results = jnp.concatenate(pieces, axis=1)
    flat_results = results.reshape(pairs_dev * capacity, head_size)
    replies = flat_results[places]
    returned = lax.all_to_all(replies, "seq", split_axis=0, concat_axis=0, tiled=True)
    return returned[position].reshape(tok, heads, head_size)


def partial_softmax(query, keys, values, scale, causal):
    rows = query.shape[0]
    span = keys.shape[0]
    size = values.shape[1] // 2
    contract = (((1,), (1,)), ((), ()))
    scores = lax.dot_general(query, keys, contract, preferred_element_type=jnp.float32)
    if causal:
        past = span - rows
        row_id = lax.broadcasted_iota(jnp.int32, (rows, rows), 0)
        col_id = lax.broadcasted_iota(jnp.int32, (rows, rows), 1)
        last = jnp.where(col_id <= row_id, scores[:, past:], NEG)
        scores = jnp.concatenate([scores[:, :past], last], axis=1) if past else last
    factor = scale * math.log2(math.e)
    peak = jnp.max(scores, axis=1, keepdims=True) * factor
    expo = jnp.exp2(scores * factor - peak).astype(jnp.bfloat16)
    out = jnp.dot(expo, values, preferred_element_type=jnp.float32)
    total = out[:, size:]
    return (out[:, :size] / total).astype(jnp.bfloat16), peak, total[:, :1]


def exchange_kernel(
    nseq, held, group, x_ref, lab_ref, out_ref, recv, qrecv, kvrecv, labs, obuf, sbuf, part, stats, merged, hot, cold,
    x_send, x_recv, q_send, q_recv, kv_send, kv_recv, l_send, l_recv, o_send, o_recv, s_send, s_recv,
    own_x, own_l, own_o, own_s, m_sem,
):
    me = lax.axis_index("seq")
    half = nseq // 2
    low = me < half
    up = me >= half
    side = me // half
    base = side * half
    mine = lax.rem(me, half)
    tok, width = x_ref.shape[1:]
    size = width // 3
    scale = 1.0 / math.sqrt(size)
    rows = group * tok
    ahead = 2
    direct = held - 1
    wide = 2 * group if half % (2 * group) == 0 else group

    def remote(src, dst, send, recv_sem, peer):
        return pltpu.make_async_remote_copy(
            src_ref=src, dst_ref=dst, send_sem=send, recv_sem=recv_sem,
            device_id={"seq": peer}, device_id_type=pl.DeviceIdType.MESH,
        )

    def x_copy(j, p):
        return remote(x_ref.at[p * held + j], recv.at[j, mine],
                      x_send.at[j, p], x_recv.at[j, mine], base + p)

    def x_arrival(j, p):
        return remote(x_ref.at[0], recv.at[j, p], x_send.at[j, p], x_recv.at[j, p], base + p)

    def q_copy(j, p):
        return remote(x_ref.at[p * held + j, :, pl.ds(0, size)], qrecv.at[j, mine],
                      q_send.at[j, p], q_recv.at[j, mine], p)

    def q_arrival(j, p):
        return remote(x_ref.at[0, :, pl.ds(0, size)], qrecv.at[j, p],
                      q_send.at[j, p], q_recv.at[j, p], half + p)

    def l_copy(peer):
        return remote(lab_ref.at[lax.rem(peer, half)], labs.at[me],
                      l_send.at[peer], l_recv.at[me], peer)

    def l_arrival(peer):
        return remote(lab_ref.at[0], labs.at[peer], l_send.at[peer], l_recv.at[peer], peer)

    def kv_copy(p):
        return remote(x_ref.at[p * held + direct, :, pl.ds(size, 2 * size)], kvrecv.at[mine],
                      kv_send.at[p], kv_recv.at[mine], half + p)

    def kv_arrival(p):
        return remote(x_ref.at[0, :, pl.ds(size, 2 * size)], kvrecv.at[p],
                      kv_send.at[p], kv_recv.at[p], p)

    def f_copy(j, p):
        return remote(obuf.at[j, base + p], out_ref.at[mine * held + j],
                      o_send.at[j, base + p], o_recv.at[side, j, mine], base + p)

    def f_arrival(j, p):
        return remote(obuf.at[j, 0], out_ref.at[p * held + j],
                      o_send.at[j, base + p], o_recv.at[side, j, p], base + p)

    def o_copy_up(j, peer):
        return remote(obuf.at[j, peer], part.at[side, mine * held + j],
                      o_send.at[j, peer], o_recv.at[side, j, mine], peer)

    def o_arrival_up(which, j, p):
        return remote(obuf.at[j, 0], part.at[which, p * held + j],
                      o_send.at[j, which * half + p], o_recv.at[which, j, p], which * half + p)

    def s_copy(j, peer):
        return remote(sbuf.at[j, peer], stats.at[side, mine, j],
                      s_send.at[j, peer], s_recv.at[side, j, mine], peer)

    def s_arrival(which, j, p):
        return remote(sbuf.at[j, 0], stats.at[which, p, j],
                      s_send.at[j, which * half + p], s_recv.at[which, j, p], which * half + p)

    def own_x_copy(j):
        return pltpu.make_async_copy(x_ref.at[mine * held + j], recv.at[j, mine], own_x.at[j])

    def own_f(j):
        return pltpu.make_async_copy(obuf.at[j, me], out_ref.at[mine * held + j], own_o.at[j])

    def own_o_up(j):
        return pltpu.make_async_copy(obuf.at[j, me], part.at[1, mine * held + j], own_o.at[j])

    def own_s_up(j):
        return pltpu.make_async_copy(sbuf.at[j, me], stats.at[1, mine, j], own_s.at[j])

    def result_copy(head):
        return pltpu.make_async_copy(merged.at[head], out_ref.at[head], m_sem.at[head])

    own_lab = pltpu.make_async_copy(lab_ref.at[mine], labs.at[me], own_l.at[0])

    def loop(start, stop, body):
        def step(k, carry):
            body(k)
            return carry

        lax.fori_loop(start, stop, step, 0)

    def each_peer(body):
        loop(1, nseq, lambda k: body(lax.rem(me + k, nseq)))

    def each_near(body):
        loop(1, half, lambda k: body(lax.rem(mine + k, half)))

    def each_far(body):
        loop(0, half, lambda k: body(lax.rem(mine + k, half)))

    own_lab.start()
    for j in range(held):
        own_x_copy(j).start()
    barrier = pltpu.get_barrier_semaphore()
    each_peer(lambda peer: pl.semaphore_signal(
        barrier, inc=1, device_id={"seq": peer}, device_id_type=pl.DeviceIdType.MESH))
    pl.semaphore_wait(barrier, nseq - 1)

    each_peer(lambda peer: l_copy(peer).start())

    def send_chunk(j):
        @pl.when(up & (j < direct))
        def _():
            each_far(lambda p: q_copy(j, p).start())

        each_near(lambda p: x_copy(j, p).start())

    loop(0, min(ahead, held), send_chunk)

    @pl.when(low)
    def _():
        each_far(lambda p: kv_copy(p).start())

    own_lab.wait()
    for j in range(held):
        own_x_copy(j).wait()
    each_peer(lambda peer: l_arrival(peer).wait_recv())

    eye = lax.broadcasted_iota(jnp.int32, (tok, tok), 0) == lax.broadcasted_iota(
        jnp.int32, (tok, tok), 1)

    def to_col(line):
        return jnp.sum(jnp.where(eye, line, jnp.zeros_like(line)), axis=1, keepdims=True)

    def to_row(col):
        return jnp.sum(jnp.where(eye, col, jnp.zeros_like(col)), axis=0, keepdims=True)

    def keep(j, first, count, result, peak, total):
        for g in range(count):
            part_rows = slice(g * tok, (g + 1) * tok)
            obuf[j, first + g] = result[part_rows]
            sbuf[j, first + g, 0:1, :] = to_row(peak[part_rows])
            sbuf[j, first + g, 1:2, :] = to_row(total[part_rows])

    def label_match(j, source):
        col = to_col(labs[source, pl.ds(j, 1), :])
        return lax.broadcasted_iota(jnp.int32, (tok, size), 1) == col

    def fill_hot(j, source):
        hot[source] = jnp.where(label_match(j, source), 1.0, 0.0).astype(jnp.bfloat16)

    def fill_cold(j, source):
        cold[source] = jnp.where(label_match(j, source), 0.0, NEG).astype(jnp.bfloat16)

    def arrive(j):
        def fill_near(p):
            fill_hot(j, base + p)
            fill_cold(j, base + p)

        loop(0, half, fill_near)
        each_near(lambda p: x_arrival(j, p).wait_recv())

    def with_ones(values):
        return jnp.concatenate([values, jnp.ones(values.shape, jnp.bfloat16)], axis=1)

    def keys_of(j, span):
        keys = recv[j, :span, :, size : 2 * size].reshape(span * tok, size)
        return jnp.concatenate(
            [keys, cold[pl.ds(base, span)].reshape(span * tok, size)], axis=1)

    def values_of(j, span):
        return with_ones(recv[j, :span, :, 2 * size :].reshape(span * tok, size))

    def causal_blocks(j, keys_low=None, values_low=None):
        for first in range(0, half, group):
            query = jnp.concatenate([
                recv[j, first : first + group, :, :size].reshape(rows, size),
                hot[pl.ds(base + first, group)].reshape(rows, size)], axis=1)
            keys, values = keys_of(j, first + group), values_of(j, first + group)
            if keys_low is not None:
                keys = jnp.concatenate([keys_low(), keys], axis=0)
                values = jnp.concatenate([values_low(), values], axis=0)
            result, peak, total = partial_softmax(query, keys, values, scale, True)
            keep(j, base + first, group, result, peak, total)

    def send_final(j):
        each_near(lambda p: f_copy(j, p).start())
        own_f(j).start()

    def chunk(j):
        arrive(j)

        @pl.when(low)
        def _():
            each_far(lambda p: q_arrival(j, p).wait_recv())

        @pl.when(j + ahead < held)
        def _():
            send_chunk(j + ahead)

        @pl.when(low)
        def _():
            loop(0, half, lambda p: fill_hot(j, half + p))
            for first in range(0, half, wide):
                query = jnp.concatenate([
                    qrecv[j, first : first + wide].reshape(wide * tok, size),
                    hot[half + first : half + first + wide].reshape(wide * tok, size)], axis=1)
                result, peak, total = partial_softmax(
                    query, keys_of(j, half), values_of(j, half), scale, False)
                keep(j, half + first, wide, result, peak, total)
                for g in range(wide):
                    o_copy_up(j, half + first + g).start()
                    s_copy(j, half + first + g).start()

        causal_blocks(j)

        @pl.when(low)
        def _():
            send_final(j)

        @pl.when(up)
        def _():
            def send_up(p):
                o_copy_up(j, half + p).start()
                s_copy(j, half + p).start()

            each_near(send_up)
            own_o_up(j).start()
            own_s_up(j).start()

    loop(0, direct, chunk)
    arrive(direct)

    @pl.when(low)
    def _():
        causal_blocks(direct)

    @pl.when(up)
    def _():
        loop(0, half, lambda p: fill_cold(direct, p))
        each_far(lambda p: kv_arrival(p).wait_recv())

        def keys_low():
            keys = kvrecv[:, :, :size].reshape(half * tok, size)
            return jnp.concatenate([keys, cold[:half].reshape(half * tok, size)], axis=1)

        def values_low():
            return with_ones(kvrecv[:, :, size:].reshape(half * tok, size))

        causal_blocks(direct, keys_low, values_low)

    send_final(direct)

    each_peer(lambda peer: l_copy(peer).wait_send())
    loop(0, held, lambda j: each_near(lambda p: x_copy(j, p).wait_send()))

    def finish_final(j):
        own_f(j).wait()

        def near(p):
            f_copy(j, p).wait_send()
            f_arrival(j, p).wait_recv()

        each_near(near)

    @pl.when(low)
    def _():
        each_far(lambda p: kv_copy(p).wait_send())

        def finish(j):
            finish_final(j)

            def far(p):
                o_copy_up(j, half + p).wait_send()
                s_copy(j, half + p).wait_send()

            each_far(far)

        loop(0, direct, finish)

    @pl.when(up)
    def _():
        loop(0, direct, lambda j: each_far(lambda p: q_copy(j, p).wait_send()))

        def finish(j):
            own_o_up(j).wait()
            own_s_up(j).wait()

            def near(p):
                o_copy_up(j, half + p).wait_send()
                s_copy(j, half + p).wait_send()
                o_arrival_up(1, j, p).wait_recv()
                s_arrival(1, j, p).wait_recv()

            each_near(near)

            def merge(p):
                o_arrival_up(0, j, p).wait_recv()
                s_arrival(0, j, p).wait_recv()
                head = p * held + j
                peak0, peak1 = stats[0, p, j, 0:1, :], stats[1, p, j, 0:1, :]
                peak = jnp.maximum(peak0, peak1)
                weight0 = stats[0, p, j, 1:2, :] * jnp.exp2(peak0 - peak)
                weight1 = stats[1, p, j, 1:2, :] * jnp.exp2(peak1 - peak)
                total = weight0 + weight1
                merged[head] = (
                    to_col(weight0 / total) * part[0, head].astype(jnp.float32)
                    + to_col(weight1 / total) * part[1, head].astype(jnp.float32)
                ).astype(jnp.bfloat16)
                result_copy(head).start()

            loop(0, half, merge)

        loop(0, direct, finish)
        loop(0, direct, lambda j: each_far(lambda p: result_copy(p * held + j).wait()))

    finish_final(direct)


def by_head(qkv, routes):
    tok, heads, width = qkv.shape
    size = width // 3
    nseq = lax.axis_size("seq")
    half = nseq // 2
    held = heads // half
    group = 2 if half % 2 == 0 else 1
    lines = jnp.transpose(routes, (1, 0)).reshape(half, held, tok)
    dma = pltpu.SemaphoreType.DMA
    out = pl.pallas_call(
        functools.partial(exchange_kernel, nseq, held, group),
        out_shape=jax.ShapeDtypeStruct((heads, tok, size), jnp.bfloat16),
        in_specs=[pl.BlockSpec(memory_space=pl.ANY)] * 2,
        out_specs=pl.BlockSpec(memory_space=pl.ANY),
        scratch_shapes=[
            pltpu.VMEM((held, half, tok, width), jnp.bfloat16),
            pltpu.VMEM((held, half, tok, size), jnp.bfloat16),
            pltpu.VMEM((half, tok, 2 * size), jnp.bfloat16),
            pltpu.VMEM((nseq, held, tok), jnp.int32),
            pltpu.VMEM((held, nseq, tok, size), jnp.bfloat16),
            pltpu.VMEM((held, nseq, 8, tok), jnp.float32),
            pltpu.VMEM((2, heads, tok, size), jnp.bfloat16),
            pltpu.VMEM((2, half, held, 8, tok), jnp.float32),
            pltpu.VMEM((heads, tok, size), jnp.bfloat16),
            pltpu.VMEM((nseq, tok, size), jnp.bfloat16),
            pltpu.VMEM((nseq, tok, size), jnp.bfloat16),
            dma((held, half)),
            dma((held, half)),
            dma((held, half)),
            dma((held, half)),
            dma((half,)),
            dma((half,)),
            dma((nseq,)),
            dma((nseq,)),
            dma((held, nseq)),
            dma((2, held, half)),
            dma((held, nseq)),
            dma((2, held, half)),
            dma((held,)),
            dma((1,)),
            dma((held,)),
            dma((held,)),
            dma((heads,)),
        ],
        compiler_params=pltpu.CompilerParams(
            collective_id=0, has_side_effects=True, vmem_limit_bytes=48 * 2**20
        ),
        name="exchange",
    )(jnp.transpose(qkv, (1, 0, 2)), lines)
    return jnp.transpose(out, (1, 0, 2))


def solution(mesh):
    placed = (P(("groups", "seq"), None, None), P(("groups", "seq"), None))
    nseq = mesh.shape["seq"]

    def local(qkv, routes):
        heads = qkv.shape[1]
        half = nseq // 2
        clusters = nseq * qkv.shape[0] // CLEN
        fits = clusters <= qkv.shape[2] // 3
        if fits and nseq % 2 == 0 and heads % half == 0:
            return by_head(qkv, routes)
        return routed(qkv, routes)

    return jax.shard_map(
        local,
        mesh=mesh,
        in_specs=placed,
        out_specs=P(("groups", "seq"), None, None),
        check_vma=False,
    )
```

```python
import functools
import math

import jax
import jax.numpy as jnp
from jax import lax
from jax.experimental import pallas as pl
from jax.experimental.pallas import tpu as pltpu
from jax.sharding import PartitionSpec as P

CLEN = 1024
NEG = -1e36


def entering(part, axis, combine, identity):
    place = lax.axis_index(axis)
    gathered = lax.all_gather(part, axis)
    state = jnp.zeros_like(part) + jnp.asarray(identity, part.dtype)

    def one(turn, state):
        return combine(state, lax.dynamic_index_in_dim(gathered, turn, 0, False))

    return lax.fori_loop(0, place, one, state)


def attend(queries, keys, values, start, scale):
    block_rows = queries.shape[1]
    span = keys.shape[1]
    scores = jnp.einsum("pqd,pkd->pqk", queries, keys, preferred_element_type=jnp.float32) * scale
    rows = start + jnp.arange(block_rows, dtype=jnp.int32)[:, None]
    cols = jnp.arange(span, dtype=jnp.int32)[None, :]
    scores = jnp.where((cols <= rows)[None], scores, -1e30)
    peak = jnp.max(scores, axis=2, keepdims=True)
    expo = jnp.exp(scores - peak)
    weights = (expo / jnp.sum(expo, axis=2, keepdims=True)).astype(jnp.bfloat16)
    return jnp.einsum("pqk,pkd->pqd", weights, values, preferred_element_type=jnp.float32).astype(
        jnp.bfloat16
    )


def routed(qkv, routes):
    tok, heads, width = qkv.shape
    head_size = width // 3
    nseq = lax.axis_size("seq")
    clusters = nseq * tok // CLEN
    pairs_dev = heads * tok // CLEN
    capacity = 3 * CLEN // 2
    block_rows = CLEN // 2
    share = CLEN // nseq
    rows_peer = pairs_dev * share
    total_pairs = heads * clusters
    scale = 1.0 / math.sqrt(head_size)
    member = routes[:, :, None] == jnp.arange(clusters, dtype=jnp.int32)[None, None, :]
    member_flat = member.reshape(tok, total_pairs)
    counts = jnp.sum(member_flat.astype(jnp.int32), axis=0)
    earlier = (jnp.arange(tok)[:, None] > jnp.arange(tok)[None, :]).astype(jnp.bfloat16)
    before = jnp.dot(earlier, member_flat.astype(jnp.bfloat16), preferred_element_type=jnp.float32)
    rank = jnp.sum(jnp.where(member, before.reshape(tok, heads, clusters), 0.0), axis=2).astype(
        jnp.int32
    )
    prefix = entering(counts, "seq", lambda first, second: first + second, jnp.zeros_like(counts))

    def lookup(table):
        return jnp.sum(jnp.where(member, table.reshape(heads, clusters)[None], 0), axis=2)

    group_counts = counts.reshape(total_pairs // pairs_dev, pairs_dev)
    within = (jnp.cumsum(group_counts, axis=1) - group_counts).reshape(total_pairs)
    slot = lookup(prefix) + rank
    pair_index = jnp.arange(heads, dtype=jnp.int32)[None, :] * clusters + routes
    owner = pair_index // pairs_dev
    local_pair = pair_index % pairs_dev
    position = (owner * rows_peer + lookup(within) + rank).reshape(tok * heads)
    target = (local_pair * capacity + slot).reshape(tok * heads)
    outgoing = (
        jnp.zeros((tok * heads, width), jnp.bfloat16)
        .at[position]
        .set(qkv.reshape(tok * heads, width))
    )
    labels = jnp.zeros((tok * heads,), jnp.int32).at[position].set(target)
    arrived, places = (
        lax.all_to_all(outgoing, "seq", split_axis=0, concat_axis=0, tiled=True),
        lax.all_to_all(labels, "seq", split_axis=0, concat_axis=0, tiled=True),
    )
    tiles = jnp.zeros((pairs_dev * capacity, width), jnp.bfloat16).at[places].set(arrived)
    tiles = tiles.reshape(pairs_dev, capacity, width)
    pieces = []
    for index in range(3):
        start = index * block_rows
        stop = start + block_rows
        pieces.append(
            attend(
                tiles[:, start:stop, :head_size],
                tiles[:, :stop, head_size : 2 * head_size],
                tiles[:, :stop, 2 * head_size :],
                start,
                scale,
            )
        )
    results = jnp.concatenate(pieces, axis=1)
    flat_results = results.reshape(pairs_dev * capacity, head_size)
    replies = flat_results[places]
    returned = lax.all_to_all(replies, "seq", split_axis=0, concat_axis=0, tiled=True)
    return returned[position].reshape(tok, heads, head_size)


def partial_softmax(query, keys, values, scale, causal):
    rows = query.shape[0]
    span = keys.shape[0]
    size = values.shape[1] // 2
    contract = (((1,), (1,)), ((), ()))
    scores = lax.dot_general(query, keys, contract, preferred_element_type=jnp.float32)
    if causal:
        past = span - rows
        row_id = lax.broadcasted_iota(jnp.int32, (rows, rows), 0)
        col_id = lax.broadcasted_iota(jnp.int32, (rows, rows), 1)
        last = jnp.where(col_id <= row_id, scores[:, past:], NEG)
        scores = jnp.concatenate([scores[:, :past], last], axis=1) if past else last
    factor = scale * math.log2(math.e)
    peak = jnp.max(scores, axis=1, keepdims=True) * factor
    expo = jnp.exp2(scores * factor - peak).astype(jnp.bfloat16)
    out = jnp.dot(expo, values, preferred_element_type=jnp.float32)
    total = out[:, size:]
    return (out[:, :size] / total).astype(jnp.bfloat16), peak, total[:, :1]


def exchange_kernel(
    nseq, held, group, x_ref, lab_ref, out_ref, recv, qrecv, labs, obuf, sbuf, part, stats, merged, hot, cold,
    x_send, x_recv, q_send, q_recv, l_send, l_recv, o_send, o_recv, s_send, s_recv,
    own_x, own_l, own_o, own_s, m_sem,
):
    me = lax.axis_index("seq")
    half = nseq // 2
    low = me < half
    up = me >= half
    side = me // half
    base = side * half
    mine = lax.rem(me, half)
    tok, width = x_ref.shape[1:]
    size = width // 3
    scale = 1.0 / math.sqrt(size)
    rows = group * tok
    ahead = 2
    wide = 2 * group if half % (2 * group) == 0 else group

    def remote(src, dst, send, recv_sem, peer):
        return pltpu.make_async_remote_copy(
            src_ref=src, dst_ref=dst, send_sem=send, recv_sem=recv_sem,
            device_id={"seq": peer}, device_id_type=pl.DeviceIdType.MESH,
        )

    def x_copy(j, p):
        return remote(x_ref.at[p * held + j], recv.at[j, mine],
                      x_send.at[j, p], x_recv.at[j, mine], base + p)

    def x_arrival(j, p):
        return remote(x_ref.at[0], recv.at[j, p], x_send.at[j, p], x_recv.at[j, p], base + p)

    def q_copy(j, p):
        return remote(x_ref.at[p * held + j, :, pl.ds(0, size)], qrecv.at[j, mine],
                      q_send.at[j, p], q_recv.at[j, mine], p)

    def q_arrival(j, p):
        return remote(x_ref.at[0, :, pl.ds(0, size)], qrecv.at[j, p],
                      q_send.at[j, p], q_recv.at[j, p], half + p)

    def l_copy(peer):
        return remote(lab_ref.at[lax.rem(peer, half)], labs.at[me],
                      l_send.at[peer], l_recv.at[me], peer)

    def l_arrival(peer):
        return remote(lab_ref.at[0], labs.at[peer], l_send.at[peer], l_recv.at[peer], peer)

    def o_copy_low(j, p):
        return remote(obuf.at[j, p], out_ref.at[mine * held + j],
                      o_send.at[j, p], o_recv.at[0, j, mine], p)

    def o_arrival_low(j, p):
        return remote(obuf.at[j, 0], out_ref.at[p * held + j],
                      o_send.at[j, p], o_recv.at[0, j, p], p)

    def o_copy_up(j, peer):
        return remote(obuf.at[j, peer], part.at[side, mine * held + j],
                      o_send.at[j, peer], o_recv.at[side, j, mine], peer)

    def o_arrival_up(which, j, p):
        return remote(obuf.at[j, 0], part.at[which, p * held + j],
                      o_send.at[j, which * half + p], o_recv.at[which, j, p], which * half + p)

    def s_copy(j, peer):
        return remote(sbuf.at[j, peer], stats.at[side, mine, j],
                      s_send.at[j, peer], s_recv.at[side, j, mine], peer)

    def s_arrival(which, j, p):
        return remote(sbuf.at[j, 0], stats.at[which, p, j],
                      s_send.at[j, which * half + p], s_recv.at[which, j, p], which * half + p)

    def own_x_copy(j):
        return pltpu.make_async_copy(x_ref.at[mine * held + j], recv.at[j, mine], own_x.at[j])

    def own_o_low(j):
        return pltpu.make_async_copy(obuf.at[j, me], out_ref.at[mine * held + j], own_o.at[j])

    def own_o_up(j):
        return pltpu.make_async_copy(obuf.at[j, me], part.at[1, mine * held + j], own_o.at[j])

    def own_s_up(j):
        return pltpu.make_async_copy(sbuf.at[j, me], stats.at[1, mine, j], own_s.at[j])

    def result_copy(head):
        return pltpu.make_async_copy(merged.at[head], out_ref.at[head], m_sem.at[head])

    own_lab = pltpu.make_async_copy(lab_ref.at[mine], labs.at[me], own_l.at[0])

    def loop(start, stop, body):
        def step(k, carry):
            body(k)
            return carry

        lax.fori_loop(start, stop, step, 0)

    def each_peer(body):
        loop(1, nseq, lambda k: body(lax.rem(me + k, nseq)))

    def each_near(body):
        loop(1, half, lambda k: body(lax.rem(mine + k, half)))

    def each_far(body):
        loop(0, half, lambda k: body(lax.rem(mine + k, half)))

    own_lab.start()
    for j in range(held):
        own_x_copy(j).start()
    barrier = pltpu.get_barrier_semaphore()
    each_peer(lambda peer: pl.semaphore_signal(
        barrier, inc=1, device_id={"seq": peer}, device_id_type=pl.DeviceIdType.MESH))
    pl.semaphore_wait(barrier, nseq - 1)

    each_near(lambda p: l_copy(base + p).start())

    @pl.when(up)
    def _():
        each_far(lambda p: l_copy(p).start())

    def send_chunk(j):
        @pl.when(up)
        def _():
            each_far(lambda p: q_copy(j, p).start())

        for k in sorted(range(1, half), key=lambda k: abs(2 * k - half)):
            x_copy(j, lax.rem(mine + k, half)).start()

    loop(0, min(ahead, held), send_chunk)
    own_lab.wait()
    for j in range(held):
        own_x_copy(j).wait()
    each_near(lambda p: l_arrival(base + p).wait_recv())

    @pl.when(low)
    def _():
        each_far(lambda p: l_arrival(half + p).wait_recv())

    eye = lax.broadcasted_iota(jnp.int32, (tok, tok), 0) == lax.broadcasted_iota(
        jnp.int32, (tok, tok), 1)

    def to_col(line):
        return jnp.sum(jnp.where(eye, line, jnp.zeros_like(line)), axis=1, keepdims=True)

    def to_row(col):
        return jnp.sum(jnp.where(eye, col, jnp.zeros_like(col)), axis=0, keepdims=True)

    def keep(j, first, count, result, peak, total):
        for g in range(count):
            part_rows = slice(g * tok, (g + 1) * tok)
            obuf[j, first + g] = result[part_rows]
            sbuf[j, first + g, 0:1, :] = to_row(peak[part_rows])
            sbuf[j, first + g, 1:2, :] = to_row(total[part_rows])

    def chunk(j):
        def label_match(source):
            col = to_col(labs[source, pl.ds(j, 1), :])
            return lax.broadcasted_iota(jnp.int32, (tok, size), 1) == col

        def fill_near(p):
            match = label_match(base + p)
            hot[base + p] = jnp.where(match, 1.0, 0.0).astype(jnp.bfloat16)
            cold[p] = jnp.where(match, 0.0, NEG).astype(jnp.bfloat16)

        loop(0, half, fill_near)
        each_near(lambda p: x_arrival(j, p).wait_recv())

        @pl.when(low)
        def _():
            each_far(lambda p: q_arrival(j, p).wait_recv())

        @pl.when(j + ahead < held)
        def _():
            send_chunk(j + ahead)

        def keys_of(span):
            keys = recv[j, :span, :, size : 2 * size].reshape(span * tok, size)
            return jnp.concatenate([keys, cold[:span].reshape(span * tok, size)], axis=1)

        def values_of(span):
            values = recv[j, :span, :, 2 * size :].reshape(span * tok, size)
            return jnp.concatenate([values, jnp.ones((span * tok, size), jnp.bfloat16)], axis=1)

        @pl.when(low)
        def _():
            def fill_far(p):
                hot[half + p] = jnp.where(label_match(half + p), 1.0, 0.0).astype(jnp.bfloat16)

            loop(0, half, fill_far)
            for first in range(0, half, wide):
                query = jnp.concatenate([
                    qrecv[j, first : first + wide].reshape(wide * tok, size),
                    hot[half + first : half + first + wide].reshape(wide * tok, size)], axis=1)
                result, peak, total = partial_softmax(
                    query, keys_of(half), values_of(half), scale, False)
                keep(j, half + first, wide, result, peak, total)
                for g in range(wide):
                    o_copy_up(j, half + first + g).start()
                    s_copy(j, half + first + g).start()

        for first in range(0, half, group):
            query = jnp.concatenate([
                recv[j, first : first + group, :, :size].reshape(rows, size),
                hot[pl.ds(base + first, group)].reshape(rows, size)], axis=1)
            result, peak, total = partial_softmax(
                query, keys_of(first + group), values_of(first + group), scale, True)
            keep(j, base + first, group, result, peak, total)

        @pl.when(low)
        def _():
            each_near(lambda p: o_copy_low(j, p).start())
            own_o_low(j).start()

        @pl.when(up)
        def _():
            def send_up(p):
                o_copy_up(j, half + p).start()
                s_copy(j, half + p).start()

            each_near(send_up)
            own_o_up(j).start()
            own_s_up(j).start()

    loop(0, held, chunk)

    each_near(lambda p: l_copy(base + p).wait_send())
    loop(0, held, lambda j: each_near(lambda p: x_copy(j, p).wait_send()))

    @pl.when(low)
    def _():
        def finish(j):
            own_o_low(j).wait()

            def near(p):
                o_copy_low(j, p).wait_send()
                o_arrival_low(j, p).wait_recv()

            def far(p):
                o_copy_up(j, half + p).wait_send()
                s_copy(j, half + p).wait_send()

            each_near(near)
            each_far(far)

        loop(0, held, finish)

    @pl.when(up)
    def _():
        each_far(lambda p: l_copy(p).wait_send())
        loop(0, held, lambda j: each_far(lambda p: q_copy(j, p).wait_send()))

        def finish(j):
            own_o_up(j).wait()
            own_s_up(j).wait()

            def near(p):
                o_copy_up(j, half + p).wait_send()
                s_copy(j, half + p).wait_send()
                o_arrival_up(1, j, p).wait_recv()
                s_arrival(1, j, p).wait_recv()

            each_near(near)

            def merge(p):
                o_arrival_up(0, j, p).wait_recv()
                s_arrival(0, j, p).wait_recv()
                head = p * held + j
                peak0, peak1 = stats[0, p, j, 0:1, :], stats[1, p, j, 0:1, :]
                peak = jnp.maximum(peak0, peak1)
                weight0 = stats[0, p, j, 1:2, :] * jnp.exp2(peak0 - peak)
                weight1 = stats[1, p, j, 1:2, :] * jnp.exp2(peak1 - peak)
                total = weight0 + weight1
                merged[head] = (
                    to_col(weight0 / total) * part[0, head].astype(jnp.float32)
                    + to_col(weight1 / total) * part[1, head].astype(jnp.float32)
                ).astype(jnp.bfloat16)
                result_copy(head).start()

            loop(0, half, merge)

        loop(0, held, finish)
        loop(0, half * held, lambda head: result_copy(head).wait())


def by_head(qkv, routes):
    tok, heads, width = qkv.shape
    size = width // 3
    nseq = lax.axis_size("seq")
    half = nseq // 2
    held = heads // half
    group = 2 if half % 2 == 0 else 1
    lines = jnp.transpose(routes, (1, 0)).reshape(half, held, tok)
    dma = pltpu.SemaphoreType.DMA
    out = pl.pallas_call(
        functools.partial(exchange_kernel, nseq, held, group),
        out_shape=jax.ShapeDtypeStruct((heads, tok, size), jnp.bfloat16),
        in_specs=[pl.BlockSpec(memory_space=pl.ANY)] * 2,
        out_specs=pl.BlockSpec(memory_space=pl.ANY),
        scratch_shapes=[
            pltpu.VMEM((held, half, tok, width), jnp.bfloat16),
            pltpu.VMEM((held, half, tok, size), jnp.bfloat16),
            pltpu.VMEM((nseq, held, tok), jnp.int32),
            pltpu.VMEM((held, nseq, tok, size), jnp.bfloat16),
            pltpu.VMEM((held, nseq, 8, tok), jnp.float32),
            pltpu.VMEM((2, heads, tok, size), jnp.bfloat16),
            pltpu.VMEM((2, half, held, 8, tok), jnp.float32),
            pltpu.VMEM((heads, tok, size), jnp.bfloat16),
            pltpu.VMEM((nseq, tok, size), jnp.bfloat16),
            pltpu.VMEM((half, tok, size), jnp.bfloat16),
            dma((held, half)),
            dma((held, half)),
            dma((held, half)),
            dma((held, half)),
            dma((nseq,)),
            dma((nseq,)),
            dma((held, nseq)),
            dma((2, held, half)),
            dma((held, nseq)),
            dma((2, held, half)),
            dma((held,)),
            dma((1,)),
            dma((held,)),
            dma((held,)),
            dma((heads,)),
        ],
        compiler_params=pltpu.CompilerParams(
            collective_id=0, has_side_effects=True, vmem_limit_bytes=48 * 2**20
        ),
        name="exchange",
    )(jnp.transpose(qkv, (1, 0, 2)), lines)
    return jnp.transpose(out, (1, 0, 2))


def solution(mesh):
    placed = (P(("groups", "seq"), None, None), P(("groups", "seq"), None))
    nseq = mesh.shape["seq"]

    def local(qkv, routes):
        heads = qkv.shape[1]
        half = nseq // 2
        clusters = nseq * qkv.shape[0] // CLEN
        fits = clusters <= qkv.shape[2] // 3
        if fits and nseq % 2 == 0 and heads % half == 0:
            return by_head(qkv, routes)
        return routed(qkv, routes)

    return jax.shard_map(
        local,
        mesh=mesh,
        in_specs=placed,
        out_specs=P(("groups", "seq"), None, None),
        check_vma=False,
    )
```
